512 devices in a mesh: dp: 8 (over z_lo, core), expert: 64 (over x, z_hi, y).
Axes of the slice: x: 4, y: 8, z: 8 (z_hi: 2, z_lo: 4; z = z_hi * 4 + z_lo), core: 2. Of those that a mesh axis runs over, the one named last changes fastest.
Arguments:
- tokens: bfloat16 [12288, 4096], P('expert', 'dp'), may hold values from -6 to 6
- cotangent: bfloat16 [12288, 4096], P('expert', 'dp'), may hold values from -6 to 6
- gate_scale: float32 [12288, 2], P('expert'), may hold values from 0.1 to 1
- expert_ids: int32 [12288, 2], P('expert'), may hold values from 0 to 47, as said below
- expert_slots: int32 [48, 2], replicated, may hold values from 0 to 63, as said below
- hot_pairs: int32 [16], replicated, may hold values from 0 to 31, as said below
- w_gate: bfloat16 [64, 4096, 1024], P('expert', 'dp'), as said below
- w_up: bfloat16 [64, 4096, 1024], P('expert', 'dp'), as said below
- w_down: bfloat16 [64, 1024, 4096], P('expert', None, 'dp'), as said below
Outputs:
- grad_tokens: bfloat16 [12288, 4096], P('expert', 'dp')
- grad_down: bfloat16 [64, 1024, 4096], P('expert', None, 'dp')
The draws below stay inside these ranges and needn't reach their ends.
Inputs may be any that keep to these rules, and one draw needn't show every extreme that they name: `expert_ids`: route k of every token names an expert whose slots have parity k. With the slot expert_slots[e, t mod 2], at most 12 routes of the tokens of one index of expert go to one slot, and in every draw some slot receives exactly 12 routes from every index. `expert_slots`: every slot belongs to exactly one expert. Both entries of a row are equal unless the expert is hot; then the second is the first plus 64 / 2. `hot_pairs`: Distinct, in no particular order; exactly the first slots of the hot experts; as many even as odd; 0 and 31 are always among them. `w_gate`: the two slots of a hot expert hold equal weights. `w_up`: the two slots of a hot expert hold equal weights. `w_down`: the two slots of a hot expert hold equal weights.
All inputs are finite; a program needn't handle non-finite values.
Results may differ from the reference program's by a relative error of at most 0.029.
Values may be sent and summed in bfloat16 or wider, within the bound.
A program may use at most 64 MiB of HBM per device.

```python
import math
import jax
import jax.numpy as jnp
from jax import lax

D = 4096
HID = 1024
TOPK = 2
TOK_DEV = 192
SLOTS = 64
HOT = 16
NEXP = 48
CAP = 12
ROWS = 768
TOKENS = 12288
N_DP = 8


def plan_slots(key):
    half_slots = SLOTS // 2
    quarter = half_slots // 2
    key_even, key_odd, key_perm, key_order = jax.random.split(jax.random.fold_in(key, 1), 4)
    even_rest = jax.random.permutation(key_even, quarter - 1)[:HOT // 2 - 1].astype(jnp.int32) + 1
    even_pick = jnp.concatenate([jnp.array([0], jnp.int32), even_rest]) * 2
    odd_rest = jax.random.permutation(key_odd, quarter - 1)[:HOT // 2 - 1].astype(jnp.int32)
    odd_pick = jnp.concatenate([jnp.array([quarter - 1], jnp.int32), odd_rest]) * 2 + 1
    hot_base = jnp.concatenate([even_pick, odd_pick]).astype(jnp.int32)
    hot_base = hot_base[jax.random.permutation(key_order, HOT)]
    base_hot = jnp.zeros((half_slots,), jnp.int32).at[hot_base].set(1)
    is_second = jnp.concatenate([jnp.zeros((half_slots,), jnp.int32), base_hot])
    hosts = jnp.argsort(is_second, stable=True)[:NEXP].astype(jnp.int32)
    first = hosts[jax.random.permutation(key_perm, NEXP)]
    second = jnp.where((first < half_slots) & (base_hot[first % half_slots] == 1), first + half_slots, first)
    slot_expert = jnp.zeros((SLOTS,), jnp.int32).at[first].set(jnp.arange(NEXP, dtype=jnp.int32))
    slot_expert = jnp.where(is_second == 1, jnp.roll(slot_expert, half_slots), slot_expert)
    return (hot_base, base_hot, is_second, first, second, slot_expert)


def route_plan(key):
    hot_base, base_hot, is_second, first, second, slot_expert = plan_slots(key)
    half_slots = SLOTS // 2
    copies = CAP // 2
    half_tok = TOK_DEV // 2
    key_full, key_blocks = jax.random.split(jax.random.fold_in(key, 2))
    slot_of = jnp.arange(half_slots, dtype=jnp.int32) * 2
    hot_first = jnp.concatenate([base_hot, jnp.zeros((half_slots,), jnp.int32)])
    drawn = (is_second[slot_of] == 0) & (hot_first[slot_of] == 0)
    full_score = jnp.where(drawn, jax.random.permutation(key_full, half_slots).astype(jnp.int32), half_slots)
    full_index = jnp.argsort(full_score, stable=True)[0].astype(jnp.int32)
    entry_index = jnp.arange(half_slots * copies, dtype=jnp.int32) // copies
    block_keys = jax.random.split(key_blocks, SLOTS * TOPK)
    families = jnp.arange(SLOTS * TOPK, dtype=jnp.int32) % TOPK
    big = half_slots * copies * 4

    def pick_half(block_key, family, allowed):
        key_score, key_rows = jax.random.split(block_key)
        score = jax.random.permutation(key_score, half_slots * copies).astype(jnp.int32)
        score = jnp.where(allowed[entry_index], score, big)
        forced = (family == 0) & (entry_index == full_index)
        score = jnp.where(forced, -1, score)
        chosen = jnp.argsort(score, stable=True)[:half_tok]
        picked = entry_index[chosen] * 2 + family
        return picked[jax.random.permutation(key_rows, half_tok)]

    def one_block(block_key, family):
        key_even, key_odd = jax.random.split(block_key)
        family_slots = jnp.arange(half_slots, dtype=jnp.int32) * 2 + family
        allow_even = is_second[family_slots] == 0
        allow_odd = hot_first[family_slots] == 0
        even_rows = pick_half(key_even, family, allow_even)
        odd_rows = pick_half(key_odd, family, allow_odd)
        return jnp.stack([even_rows, odd_rows], axis=1).reshape(TOK_DEV)
    slots = jax.vmap(one_block)(block_keys, families).reshape(SLOTS, TOPK, TOK_DEV)
    slots = jnp.transpose(slots, (0, 2, 1)).reshape(TOKENS, TOPK)
    return slot_expert[slots]


def draw_expert_ids(key, part):
    return route_plan(key)


def draw_expert_slots(key, part):
    hot_base, base_hot, is_second, first, second, slot_expert = plan_slots(key)
    return jnp.stack([first, second], axis=1)


def draw_hot_pairs(key, part):
    hot_base, base_hot, is_second, first, second, slot_expert = plan_slots(key)
    return hot_base


def slot_weights(key, shape, fan_in, is_second):
    values = jax.random.normal(key, shape, jnp.float32)
    values = values * fan_in ** (-0.5)
    values = jnp.where(is_second[:, None, None] == 1, jnp.roll(values, SLOTS // 2, axis=0), values)
    return values.astype(jnp.bfloat16)


def draw_w_gate(key, part):
    hot_base, base_hot, is_second, first, second, slot_expert = plan_slots(key)
    key = jax.random.fold_in(key, 11)
    return slot_weights(key, (SLOTS, D, HID), D, is_second)


def draw_w_up(key, part):
    hot_base, base_hot, is_second, first, second, slot_expert = plan_slots(key)
    key = jax.random.fold_in(key, 12)
    return slot_weights(key, (SLOTS, D, HID), D, is_second)


def draw_w_down(key, part):
    hot_base, base_hot, is_second, first, second, slot_expert = plan_slots(key)
    key = jax.random.fold_in(key, 13)
    return slot_weights(key, (SLOTS, HID, D), HID, is_second)


def block_scale(rng, extent, cuts, least, top_value):
    def one(axis_at, blocks):
        draws = jax.random.uniform(jax.random.fold_in(jax.random.fold_in(rng, 6), axis_at), (blocks,), jnp.float32, least / len(cuts), top_value / len(cuts))
        return jnp.repeat(jnp.exp(draws), extent[axis_at] // blocks).reshape((-1,) + (1,) * (len(extent) - axis_at - 1))

    gain = one(*cuts[0])
    for cut in cuts[1:]:
        gain = gain * one(*cut)
    return gain


def bell_draw(own_key, extent, width, bound, cuts=(), held_as=jnp.bfloat16):
    values = width * jax.random.normal(own_key, extent, jnp.float32)
    if cuts:
        values = values * block_scale(own_key, extent, cuts, -0.22, 0.18)
    return jnp.clip(values, -bound, bound).astype(held_as)


def setup_inputs(seed: int = 0) -> dict:
    key_list = jax.random.split(jax.random.key(seed), 10)
    tokens = bell_draw(key_list[0], (TOKENS, D), 1.0, 6.0, ((0, 64), (1, 8)))
    cotangent = bell_draw(key_list[1], (TOKENS, D), 1.0, 6.0, ((0, 64), (1, 8)))
    gate_scale = jnp.clip(jnp.exp(math.log(1.0) - 2.3025851 * jax.random.uniform(key_list[2], (TOKENS, TOPK), jnp.float32) ** block_scale(key_list[2], (TOKENS, TOPK), ((0, 64),), -0.2, 0.2)), 0.1, 1.0)
    expert_ids = draw_expert_ids(jax.random.fold_in(key_list[9], 71), 0)
    expert_slots = draw_expert_slots(jax.random.fold_in(key_list[9], 71), 0)
    hot_pairs = draw_hot_pairs(jax.random.fold_in(key_list[9], 71), 0)
    w_gate = draw_w_gate(jax.random.fold_in(key_list[9], 71), 0)
    w_up = draw_w_up(jax.random.fold_in(key_list[9], 71), 0)
    w_down = draw_w_down(jax.random.fold_in(key_list[9], 71), 0)
    return dict(tokens=tokens, cotangent=cotangent, gate_scale=gate_scale, expert_ids=expert_ids, expert_slots=expert_slots, hot_pairs=hot_pairs, w_gate=w_gate, w_up=w_up, w_down=w_down)


def swiglu_back(gate_sum, up_sum, grad_hidden):
    sigmoid_gate = jax.nn.sigmoid(gate_sum)
    active = gate_sum * sigmoid_gate
    hidden = (active * up_sum).astype(jnp.bfloat16)
    grad_up = (grad_hidden * active).astype(jnp.bfloat16)
    grad_gate = (grad_hidden * up_sum * sigmoid_gate * (1.0 + gate_sum * (1.0 - sigmoid_gate))).astype(jnp.bfloat16)
    return hidden, grad_gate, grad_up


def block_sum(rows, weight):
    parts = jnp.einsum("rbd,bdh->rbh", rows.reshape(rows.shape[0], N_DP, -1).astype(jnp.float32),
                       weight.reshape(N_DP, -1, weight.shape[1]).astype(jnp.float32))
    rounded = lax.optimization_barrier(parts.astype(jnp.bfloat16))
    return jnp.sum(rounded.astype(jnp.float32), axis=1)


def reference(tokens, cotangent, gate_scale, expert_ids, expert_slots, hot_pairs, w_gate, w_up, w_down):
    total = TOKENS * TOPK
    half_slots = SLOTS // 2
    parity = (jnp.arange(TOKENS, dtype=jnp.int32) % 2)[:, None]
    route_slot = jnp.where(parity == 1, expert_slots[expert_ids, 1], expert_slots[expert_ids, 0]).reshape(total).astype(jnp.int32)
    token_index = jnp.arange(total, dtype=jnp.int32) // TOPK
    scaled = (gate_scale[:, :, None] * cotangent[:, None, :].astype(jnp.float32)).astype(jnp.bfloat16).reshape(total, D)
    span = 2 * ROWS

    def per_slot(carry, slot):
        partner = (slot + half_slots) % SLOTS
        hot_flag = jnp.any(hot_pairs == slot % half_slots)
        member = (route_slot == slot) | (hot_flag & (route_slot == partner))
        sort_keys = jnp.where(member, jnp.arange(total, dtype=jnp.int32), total)
        row_order = jnp.argsort(sort_keys)[:span].astype(jnp.int32)
        is_valid = member[row_order]
        rows_x = jnp.where(is_valid[:, None], tokens[token_index[row_order]], 0).astype(jnp.bfloat16)
        rows_dy = jnp.where(is_valid[:, None], scaled[row_order], 0).astype(jnp.bfloat16)
        gate_sum = block_sum(rows_x, w_gate[slot])
        up_sum = block_sum(rows_x, w_up[slot])
        grad_hidden = block_sum(rows_dy, w_down[slot].T)
        hidden, grad_gate, grad_up = swiglu_back(gate_sum, up_sum, grad_hidden)
        route_grad = (jnp.dot(grad_gate, w_gate[slot].T, preferred_element_type=jnp.float32)
                      + jnp.dot(grad_up, w_up[slot].T, preferred_element_type=jnp.float32)).astype(jnp.bfloat16)
        mine = is_valid & (route_slot[row_order] == slot)
        carry = carry.at[token_index[row_order]].add(jnp.where(mine[:, None], route_grad.astype(jnp.float32), 0.0))
        grad_down = jnp.dot(hidden.T, rows_dy, preferred_element_type=jnp.float32).astype(jnp.bfloat16)
        return carry, grad_down

    start = jnp.zeros((TOKENS, D), jnp.float32)
    summed, grad_down = lax.scan(per_slot, start, jnp.arange(SLOTS, dtype=jnp.int32))
    return summed.astype(jnp.bfloat16), grad_down
```

```python
import jax
import jax.numpy as jnp
from jax import lax
from jax.experimental import pallas as pl
from jax.experimental.pallas import tpu as pltpu
from jax.sharding import PartitionSpec as P

BF = jnp.bfloat16
F32 = jnp.float32
MESH = pl.DeviceIdType.MESH
CHUNK = 32


def swiglu_back(gate_sum, up_sum, grad_hidden):
    sigmoid_gate = jax.nn.sigmoid(gate_sum)
    active = gate_sum * sigmoid_gate
    hidden = (active * up_sum).astype(BF)
    grad_up = (grad_hidden * active).astype(BF)
    grad_gate = (
        grad_hidden * up_sum * sigmoid_gate * (1.0 + gate_sum * (1.0 - sigmoid_gate))
    ).astype(BF)
    return (hidden, grad_gate, grad_up)


def dot_last(left, right):
    return lax.dot_general(left, right, (((1,), (1,)), ((), ())), preferred_element_type=F32)


def dot_first(left, right):
    return lax.dot_general(left, right, (((0,), (0,)), ((), ())), preferred_element_type=F32)


def expert_kernel(
    x_ref, dy_ref, wg_ref, wu_ref, wd_ref, route_ref, own_ref,
    part, from_sib, from_prev, done,
    s_sib, r_sib, s_rs, r_rs, s_ag, r_ag, s_fin, r_fin,
):
    rows, hid = x_ref.shape[0], wg_ref.shape[1]
    half = rows // 2
    count = half // (2 * CHUNK)
    chips = lax.axis_size("dp") // 2
    last = chips - 1
    me = lax.axis_index("dp")
    core = lax.rem(me, 2)
    chip = lax.div(me, 2)
    sib = {"dp": me + 1 - 2 * core}

    barrier = pltpu.get_barrier_semaphore()
    pl.semaphore_signal(barrier, inc=1, device_id=sib, device_id_type=MESH)

    @pl.when(chip > 0)
    def _():
        pl.semaphore_signal(barrier, inc=1, device_id={"dp": me - 2}, device_id_type=MESH)

    @pl.when(chip < last)
    def _():
        pl.semaphore_signal(barrier, inc=1, device_id={"dp": me + 2}, device_id_type=MESH)

    inner = (chip > 0) & (chip < last)

    @pl.when(inner)
    def _():
        pl.semaphore_wait(barrier, 3)

    @pl.when(jnp.logical_not(inner))
    def _():
        pl.semaphore_wait(barrier, 2)

    def at(f, k):
        return pl.multiple_of((f * count + k) * CHUNK, CHUNK)

    def own_rows(f, k):
        return pl.ds(pl.multiple_of(core * half + at(f, k), CHUNK), CHUNK)

    def sib_rows(f, k):
        return pl.ds(pl.multiple_of((1 - core) * half + at(f, k), CHUNK), CHUNK)

    def buf_rows(f, k):
        return pl.ds(at(f, k), CHUNK)

    def send_sib(f, k):
        return pltpu.make_async_remote_copy(
            src_ref=part.at[sib_rows(f, k)], dst_ref=from_sib.at[buf_rows(f, k)],
            send_sem=s_sib.at[f, k], recv_sem=r_sib.at[f, k],
            device_id=sib, device_id_type=MESH,
        )

    def send_rs(f, k):
        nxt = {"dp": me + 2 if f == 0 else me - 2}
        return pltpu.make_async_remote_copy(
            src_ref=part.at[own_rows(f, k)], dst_ref=from_prev.at[buf_rows(f, k)],
            send_sem=s_rs.at[f, k], recv_sem=r_rs.at[f, k],
            device_id=nxt, device_id_type=MESH,
        )

    def send_ag(f, k):
        prev = {"dp": me - 2 if f == 0 else me + 2}
        return pltpu.make_async_remote_copy(
            src_ref=done.at[own_rows(f, k)], dst_ref=done.at[own_rows(f, k)],
            send_sem=s_ag.at[f, k], recv_sem=r_ag.at[f, k],
            device_id=prev, device_id_type=MESH,
        )

    def send_fin(f, k):
        return pltpu.make_async_remote_copy(
            src_ref=done.at[own_rows(f, k)], dst_ref=done.at[own_rows(f, k)],
            send_sem=s_fin.at[f, k], recv_sem=r_fin.at[f, k],
            device_id=sib, device_id_type=MESH,
        )

    def parts_of(which):
        here = pl.ds(pl.multiple_of(which * half, CHUNK), half)

        @pl.loop(0, hid // 256)
        def _(j):
            cols = pl.ds(pl.multiple_of(j * 256, 256), 256)
            x = x_ref[here, :]
            dy = dy_ref[here, :]
            part[here, pl.ds(pl.multiple_of(j * 256, 256), 256)] = jnp.dot(
                x, wg_ref[:, cols], preferred_element_type=F32
            ).astype(BF)
            part[here, pl.ds(pl.multiple_of(hid + j * 256, 256), 256)] = jnp.dot(
                x, wu_ref[:, cols], preferred_element_type=F32
            ).astype(BF)
            part[here, pl.ds(pl.multiple_of(2 * hid + j * 256, 256), 256)] = dot_last(
                dy, wd_ref[cols, :]
            ).astype(BF)

    parts_of(1 - core)

    @pl.loop(0, count)
    def _(k):
        for f in range(2):
            send_sib(f, k).start()

    parts_of(core)

    @pl.loop(0, count + 2 * last)
    def _(tick):
        for f in range(2):
            q = chip if f == 0 else last - chip
            k = tick - q

            @pl.when((k >= 0) & (k < count))
            def _():
                send_sib(f, k).wait_recv()
                mine = own_rows(f, k)

                @pl.when(q == 0)
                def _():
                    for c in range(3):
                        cols = pl.ds(c * hid, hid)
                        part[mine, cols] = (
                            part[mine, cols].astype(F32)
                            + from_sib[buf_rows(f, k), cols].astype(F32)
                        ).astype(BF)

                @pl.when(q > 0)
                def _():
                    send_rs(f, k).wait_recv()

                @pl.when((q > 0) & (q < last))
                def _():
                    for c in range(3):
                        cols = pl.ds(c * hid, hid)
                        part[mine, cols] = (
                            part[mine, cols].astype(F32)
                            + from_sib[buf_rows(f, k), cols].astype(F32)
                            + from_prev[buf_rows(f, k), cols].astype(F32)
                        ).astype(BF)

                @pl.when(q < last)
                def _():
                    send_rs(f, k).start()

                @pl.when(q == last)
                def _():
                    sums = []
                    for c in range(3):
                        cols = pl.ds(c * hid, hid)
                        sums.append(
                            part[mine, cols].astype(F32)
                            + from_sib[buf_rows(f, k), cols].astype(F32)
                            + from_prev[buf_rows(f, k), cols].astype(F32)
                        )
                    for c, value in enumerate(swiglu_back(*sums)):
                        done[mine, pl.ds(c * hid, hid)] = value
                    send_ag(f, k).start()
                    send_fin(f, k).start()

        for f in range(2):
            q = chip if f == 0 else last - chip
            k = tick - 2 * last + q

            @pl.when((q < last) & (k >= 0) & (k < count))
            def _():
                send_ag(f, k).wait_recv()

                @pl.when(q > 0)
                def _():
                    send_ag(f, k).start()

                send_fin(f, k).start()

    @pl.loop(0, count)
    def _(k):
        for f in range(2):
            q = chip if f == 0 else last - chip
            send_fin(f, k).wait_recv()
            send_sib(f, k).wait_send()
            send_fin(f, k).wait_send()

            @pl.when(q < last)
            def _():
                send_rs(f, k).wait_send()

            @pl.when(q > 0)
            def _():
                send_ag(f, k).wait_send()

    block = rows // 4

    @pl.loop(0, 4)
    def _(j):
        here = pl.ds(pl.multiple_of(j * block, 64), block)
        route_ref[here, :] = (
            dot_last(done[here, pl.ds(hid, hid)], wg_ref[...])
            + dot_last(done[here, pl.ds(2 * hid, hid)], wu_ref[...])
        ).astype(BF)

    @pl.loop(0, hid // 256)
    def _(j):
        cols = pl.ds(pl.multiple_of(j * 256, 256), 256)
        own_ref[cols, :] = dot_first(done[:, cols], dy_ref[...])


def expert_call(rows_x, rows_dy, w_gate, w_up, w_down):
    rows, width = rows_x.shape
    hid = w_gate.shape[1]
    half = rows // 2
    count = half // (2 * CHUNK)
    sems = [pltpu.SemaphoreType.DMA((2, count))] * 8
    return pl.pallas_call(
        expert_kernel,
        out_shape=(
            jax.ShapeDtypeStruct((rows, width), BF),
            jax.ShapeDtypeStruct((hid, width), F32),
        ),
        in_specs=[pl.BlockSpec(memory_space=pltpu.VMEM)] * 5,
        out_specs=[pl.BlockSpec(memory_space=pltpu.VMEM)] * 2,
        scratch_shapes=[
            pltpu.VMEM((rows, 3 * hid), BF),
            pltpu.VMEM((half, 3 * hid), BF),
            pltpu.VMEM((half, 3 * hid), BF),
            pltpu.VMEM((rows, 3 * hid), BF),
        ] + sems,
        compiler_params=pltpu.CompilerParams(
            collective_id=0, has_side_effects=True, vmem_limit_bytes=50 * 1024 * 1024
        ),
        cost_estimate=pl.CostEstimate(
            flops=12 * rows * width * hid, bytes_accessed=8 * 1024 * 1024, transcendentals=0
        ),
        name="expert_sums",
    )(rows_x, rows_dy, w_gate, w_up, w_down)


def from_partner(block, axis, stride):
    count = lax.axis_size(axis)
    route = []
    for low in range(count):
        high = low | 1 << stride
        if high != low and high < count:
            route += [(low, high), (high, low)]
    return lax.ppermute(block, axis, route)


def contract_first(left, right):
    return lax.dot_general(
        left, right, (((0,), (0,)), ((), ())), preferred_element_type=jnp.float32
    )


def on_device(
    tokens, cotangent, gate_scale, expert_ids, expert_slots, hot_pairs, w_gate, w_up, w_down
):
    tok_rows, width = tokens.shape
    route_count = expert_ids.shape[1]
    slot_count = lax.axis_size("expert")
    capacity = 2 * tok_rows * route_count // slot_count
    entries = tok_rows * route_count
    expert_iota = jnp.arange(expert_slots.shape[0], dtype=jnp.int32)
    expert_match = expert_ids[:, :, None] == expert_iota
    parity = (jnp.arange(tok_rows, dtype=jnp.int32) % 2)[:, None, None]
    slot_table = jnp.where(parity == 1, expert_slots[:, 1], expert_slots[:, 0])
    route_slot = jnp.sum(jnp.where(expert_match, slot_table, 0), axis=2).reshape(entries)
    slot_hit = (route_slot[:, None] == jnp.arange(slot_count, dtype=jnp.int32)).astype(jnp.int32)
    before = jnp.cumsum(slot_hit, axis=0) - slot_hit
    target = route_slot * capacity + jnp.sum(before * slot_hit, axis=1)
    placing = (
        jnp.arange(slot_count * capacity, dtype=jnp.int32)[:, None] == target[None, :]
    ).astype(jnp.bfloat16)
    repeated = jnp.broadcast_to(tokens[:, None, :], (tok_rows, route_count, width)).reshape(
        entries, width
    )
    scaled = (
        (gate_scale[:, :, None] * cotangent[:, None, :].astype(jnp.float32))
        .astype(jnp.bfloat16)
        .reshape(entries, width)
    )
    send_x = (
        jnp.dot(placing, repeated, preferred_element_type=jnp.float32)
        .astype(jnp.bfloat16)
        .reshape(slot_count, capacity, width)
    )
    send_dy = (
        jnp.dot(placing, scaled, preferred_element_type=jnp.float32)
        .astype(jnp.bfloat16)
        .reshape(slot_count, capacity, width)
    )
    recv_x, recv_dy = (
        lax.all_to_all(send_x, "expert", split_axis=0, concat_axis=0, tiled=True),
        lax.all_to_all(send_dy, "expert", split_axis=0, concat_axis=0, tiled=True),
    )
    rows_x = recv_x.reshape(-1, width)
    rows_dy = recv_dy.reshape(-1, width)
    gate_weight = w_gate[0]
    up_weight = w_up[0]
    down_weight = w_down[0]
    route_grad, own_grad = expert_call(rows_x, rows_dy, gate_weight, up_weight, down_weight)
    returned = lax.all_to_all(
        route_grad.reshape(slot_count, capacity, width),
        "expert",
        split_axis=0,
        concat_axis=0,
        tiled=True,
    )
    per_route = contract_first(placing, returned.reshape(-1, width))
    grad_tokens = jnp.sum(per_route.reshape(tok_rows, route_count, width), axis=1).astype(
        jnp.bfloat16
    )
    pair_bit = slot_count.bit_length() - 2
    half_slots = slot_count // 2
    hot_flag = jnp.any(hot_pairs == lax.axis_index("expert") % half_slots).astype(jnp.float32)
    partner = from_partner(own_grad.astype(jnp.bfloat16), "expert", pair_bit).astype(own_grad.dtype)
    grad_down = (own_grad + hot_flag * partner).astype(jnp.bfloat16)[None]
    return (grad_tokens, grad_down)


def solution(mesh):
    placed = (
        P("expert", "dp"),
        P("expert", "dp"),
        P("expert", None),
        P("expert", None),
        P(),
        P(),
        P("expert", "dp", None),
        P("expert", "dp", None),
        P("expert", None, "dp"),
    )
    return jax.shard_map(
        on_device,
        mesh=mesh,
        in_specs=placed,
        out_specs=(P("expert", "dp"), P("expert", None, "dp")),
        check_vma=False,
    )
```

```python
import jax
import jax.numpy as jnp
import numpy as np
from jax import lax
from jax.experimental import pallas as pl
from jax.experimental.pallas import tpu as pltpu
from jax.sharding import PartitionSpec as P

BF = jnp.bfloat16
F32 = jnp.float32
MESH = pl.DeviceIdType.MESH
CHUNK = 32
PIECE = 48
CAP = 12
NX = 4
NY = 8


def swiglu_back(gate_sum, up_sum, grad_hidden):
    sigmoid_gate = jax.nn.sigmoid(gate_sum)
    active = gate_sum * sigmoid_gate
    hidden = (active * up_sum).astype(BF)
    grad_up = (grad_hidden * active).astype(BF)
    grad_gate = (
        grad_hidden * up_sum * sigmoid_gate * (1.0 + gate_sum * (1.0 - sigmoid_gate))
    ).astype(BF)
    return (hidden, grad_gate, grad_up)


def dot_last(left, right):
    return lax.dot_general(left, right, (((1,), (1,)), ((), ())), preferred_element_type=F32)


def dot_first(left, right):
    return lax.dot_general(left, right, (((0,), (0,)), ((), ())), preferred_element_type=F32)


def expert_kernel(
    x_ref, dy_ref, wg_ref, wu_ref, wd_ref, route_ref, own_ref,
    part, from_sib, from_prev, done,
    s_sib, r_sib, s_rs, r_rs, s_ag, r_ag, s_fin, r_fin,
):
    rows, hid = x_ref.shape[0], wg_ref.shape[1]
    half = rows // 2
    count = half // (2 * CHUNK)
    chips = lax.axis_size("dp") // 2
    last = chips - 1
    me = lax.axis_index("dp")
    core = lax.rem(me, 2)
    chip = lax.div(me, 2)
    sib = {"dp": me + 1 - 2 * core}

    barrier = pltpu.get_barrier_semaphore()
    pl.semaphore_signal(barrier, inc=1, device_id=sib, device_id_type=MESH)

    @pl.when(chip > 0)
    def _():
        pl.semaphore_signal(barrier, inc=1, device_id={"dp": me - 2}, device_id_type=MESH)

    @pl.when(chip < last)
    def _():
        pl.semaphore_signal(barrier, inc=1, device_id={"dp": me + 2}, device_id_type=MESH)

    inner = (chip > 0) & (chip < last)

    @pl.when(inner)
    def _():
        pl.semaphore_wait(barrier, 3)

    @pl.when(jnp.logical_not(inner))
    def _():
        pl.semaphore_wait(barrier, 2)

    def at(f, k):
        return pl.multiple_of((f * count + k) * CHUNK, CHUNK)

    def own_rows(f, k):
        return pl.ds(pl.multiple_of(core * half + at(f, k), CHUNK), CHUNK)

    def sib_rows(f, k):
        return pl.ds(pl.multiple_of((1 - core) * half + at(f, k), CHUNK), CHUNK)

    def buf_rows(f, k):
        return pl.ds(at(f, k), CHUNK)

    def send_sib(f, k):
        return pltpu.make_async_remote_copy(
            src_ref=part.at[sib_rows(f, k)], dst_ref=from_sib.at[buf_rows(f, k)],
            send_sem=s_sib.at[f, k], recv_sem=r_sib.at[f, k],
            device_id=sib, device_id_type=MESH,
        )

    def send_rs(f, k):
        nxt = {"dp": me + 2 if f == 0 else me - 2}
        return pltpu.make_async_remote_copy(
            src_ref=part.at[own_rows(f, k)], dst_ref=from_prev.at[buf_rows(f, k)],
            send_sem=s_rs.at[f, k], recv_sem=r_rs.at[f, k],
            device_id=nxt, device_id_type=MESH,
        )

    def send_ag(f, k):
        prev = {"dp": me - 2 if f == 0 else me + 2}
        return pltpu.make_async_remote_copy(
            src_ref=done.at[own_rows(f, k)], dst_ref=done.at[own_rows(f, k)],
            send_sem=s_ag.at[f, k], recv_sem=r_ag.at[f, k],
            device_id=prev, device_id_type=MESH,
        )

    def send_fin(f, k):
        return pltpu.make_async_remote_copy(
            src_ref=done.at[own_rows(f, k)], dst_ref=done.at[own_rows(f, k)],
            send_sem=s_fin.at[f, k], recv_sem=r_fin.at[f, k],
            device_id=sib, device_id_type=MESH,
        )

    def parts_of(which):
        here = pl.ds(pl.multiple_of(which * half, CHUNK), half)

        @pl.loop(0, hid // 256)
        def _(j):
            cols = pl.ds(pl.multiple_of(j * 256, 256), 256)
            x = x_ref[here, :]
            dy = dy_ref[here, :]
            part[here, pl.ds(pl.multiple_of(j * 256, 256), 256)] = jnp.dot(
                x, wg_ref[:, cols], preferred_element_type=F32
            ).astype(BF)
            part[here, pl.ds(pl.multiple_of(hid + j * 256, 256), 256)] = jnp.dot(
                x, wu_ref[:, cols], preferred_element_type=F32
            ).astype(BF)
            part[here, pl.ds(pl.multiple_of(2 * hid + j * 256, 256), 256)] = dot_last(
                dy, wd_ref[cols, :]
            ).astype(BF)

    parts_of(1 - core)

    @pl.loop(0, count)
    def _(k):
        for f in range(2):
            send_sib(f, k).start()

    parts_of(core)

    @pl.loop(0, count + 2 * last)
    def _(tick):
        for f in range(2):
            q = chip if f == 0 else last - chip
            k = tick - q

            @pl.when((k >= 0) & (k < count))
            def _():
                send_sib(f, k).wait_recv()
                mine = own_rows(f, k)

                @pl.when(q == 0)
                def _():
                    for c in range(3):
                        cols = pl.ds(c * hid, hid)
                        part[mine, cols] = (
                            part[mine, cols].astype(F32)
                            + from_sib[buf_rows(f, k), cols].astype(F32)
                        ).astype(BF)

                @pl.when(q > 0)
                def _():
                    send_rs(f, k).wait_recv()

                @pl.when((q > 0) & (q < last))
                def _():
                    for c in range(3):
                        cols = pl.ds(c * hid, hid)
                        part[mine, cols] = (
                            part[mine, cols].astype(F32)
                            + from_sib[buf_rows(f, k), cols].astype(F32)
                            + from_prev[buf_rows(f, k), cols].astype(F32)
                        ).astype(BF)

                @pl.when(q < last)
                def _():
                    send_rs(f, k).start()

                @pl.when(q == last)
                def _():
                    sums = []
                    for c in range(3):
                        cols = pl.ds(c * hid, hid)
                        sums.append(
                            part[mine, cols].astype(F32)
                            + from_sib[buf_rows(f, k), cols].astype(F32)
                            + from_prev[buf_rows(f, k), cols].astype(F32)
                        )
                    for c, value in enumerate(swiglu_back(*sums)):
                        done[mine, pl.ds(c * hid, hid)] = value
                    send_ag(f, k).start()
                    send_fin(f, k).start()

        for f in range(2):
            q = chip if f == 0 else last - chip
            k = tick - 2 * last + q

            @pl.when((q < last) & (k >= 0) & (k < count))
            def _():
                send_ag(f, k).wait_recv()

                @pl.when(q > 0)
                def _():
                    send_ag(f, k).start()

                send_fin(f, k).start()

    @pl.loop(0, count)
    def _(k):
        for f in range(2):
            q = chip if f == 0 else last - chip
            send_fin(f, k).wait_recv()
            send_sib(f, k).wait_send()
            send_fin(f, k).wait_send()

            @pl.when(q < last)
            def _():
                send_rs(f, k).wait_send()

            @pl.when(q > 0)
            def _():
                send_ag(f, k).wait_send()

    block = rows // 4

    @pl.loop(0, 4)
    def _(j):
        here = pl.ds(pl.multiple_of(j * block, 64), block)
        route_ref[here, :] = (
            dot_last(done[here, pl.ds(hid, hid)], wg_ref[...])
            + dot_last(done[here, pl.ds(2 * hid, hid)], wu_ref[...])
        ).astype(BF)

    @pl.loop(0, hid // 256)
    def _(j):
        cols = pl.ds(pl.multiple_of(j * 256, 256), 256)
        own_ref[cols, :] = dot_first(done[:, cols], dy_ref[...])


def expert_call(rows_x, rows_dy, w_gate, w_up, w_down):
    rows, width = rows_x.shape
    hid = w_gate.shape[1]
    half = rows // 2
    count = half // (2 * CHUNK)
    sems = [pltpu.SemaphoreType.DMA((2, count))] * 8
    return pl.pallas_call(
        expert_kernel,
        out_shape=(
            jax.ShapeDtypeStruct((rows, width), BF),
            jax.ShapeDtypeStruct((hid, width), F32),
        ),
        in_specs=[pl.BlockSpec(memory_space=pltpu.VMEM)] * 5,
        out_specs=[pl.BlockSpec(memory_space=pltpu.VMEM)] * 2,
        scratch_shapes=[
            pltpu.VMEM((rows, 3 * hid), BF),
            pltpu.VMEM((half, 3 * hid), BF),
            pltpu.VMEM((half, 3 * hid), BF),
            pltpu.VMEM((rows, 3 * hid), BF),
        ] + sems,
        compiler_params=pltpu.CompilerParams(
            collective_id=0, has_side_effects=True, vmem_limit_bytes=50 * 1024 * 1024
        ),
        cost_estimate=pl.CostEstimate(
            flops=12 * rows * width * hid, bytes_accessed=8 * 1024 * 1024, transcendentals=0
        ),
        name="expert_sums",
    )(rows_x, rows_dy, w_gate, w_up, w_down)


def coords():
    spot = lax.axis_index("expert")
    dp = lax.axis_index("dp")
    y = lax.rem(spot, NY)
    z_hi = lax.rem(lax.div(spot, NY), 2)
    x = lax.div(spot, 2 * NY)
    z_lo = lax.div(dp, 2)
    return x, z_hi, y, z_hi * 4 + z_lo, lax.rem(dp, 2)


def at_place(x, y, z, core):
    return {
        "dp": lax.rem(z, 4) * 2 + core,
        "expert": (x * 2 + lax.div(z, 4)) * NY + y,
    }


def plane_target(x, z_hi, y):
    return {"expert": (x * 2 + z_hi) * NY + y}


def signal_all(barrier, places):
    for place in places:
        pl.semaphore_signal(barrier, inc=1, device_id=place, device_id_type=MESH)


def signal_plane(barrier, x, z_hi, y):
    @pl.loop(1, NX * NY)
    def _(step):
        there = lax.rem(x * NY + y + step, NX * NY)
        pl.semaphore_signal(
            barrier, inc=1,
            device_id=plane_target(lax.div(there, NY), z_hi, lax.rem(there, NY)),
            device_id_type=MESH,
        )


def column_of(row):
    n = row.shape[1]
    diagonal = lax.broadcasted_iota(jnp.int32, (n, n), 0) == lax.broadcasted_iota(
        jnp.int32, (n, n), 1
    )
    return jnp.sum(jnp.where(diagonal, row, 0.0), axis=1, keepdims=True)


def route_targets(ids_ref, slots_ref, slot_count, capacity):
    tok = ids_ref.shape[1]
    experts = slots_ref.shape[0]
    odd = lax.broadcasted_iota(jnp.int32, (experts, tok), 1) % 2 == 1
    table = jnp.where(odd, slots_ref[:, 1:2], slots_ref[:, 0:1])
    expert_row = lax.broadcasted_iota(jnp.int32, (experts, tok), 0)
    slot_row = lax.broadcasted_iota(jnp.int32, (slot_count, tok), 0)
    slots = [
        jnp.sum(jnp.where(ids_ref[k : k + 1, :] == expert_row, table, 0), axis=0, keepdims=True)
        for k in range(2)
    ]
    hits = [jnp.where(slot == slot_row, 1.0, 0.0) for slot in slots]
    earlier = lax.broadcasted_iota(jnp.int32, (tok, tok), 0) < lax.broadcasted_iota(
        jnp.int32, (tok, tok), 1
    )
    before = jnp.dot(
        (hits[0] + hits[1]).astype(BF),
        jnp.where(earlier, 1.0, 0.0).astype(BF),
        preferred_element_type=F32,
    )
    return [
        slot.astype(F32) * capacity + jnp.sum(hit * before, axis=0, keepdims=True)
        for slot, hit in zip(slots, hits)
    ]


def dispatch_kernel(
    tok_ref, cot_ref, scale_ref, ids_ref, slots_ref, codes_ref, perm_ref,
    rows_x_ref, rows_dy_ref,
    relay, far, meta, far_meta, scaled, send, land,
    s_one, r_one, s_two, r_two, s_meta, r_meta, s_xy, r_xy,
):
    tok, width = tok_ref.shape
    slot_count = NX * 2 * NY
    capacity = CAP
    wide = width // 2
    message = 4 * capacity
    x, z_hi, y, z, core = coords()
    plane = NX * NY
    here = x * NY + y
    up = at_place(x, y, lax.rem(z + 2, 8), core)
    down = at_place(x, y, lax.rem(z + 6, 8), core)
    across = at_place(x, y, lax.rem(z + 4, 8), core)
    pieces = tok // PIECE

    barrier = pltpu.get_barrier_semaphore()
    signal_all(barrier, (up, down, across))
    signal_plane(barrier, x, z_hi, y)
    targets = route_targets(ids_ref, slots_ref, slot_count, capacity)
    meta[...] = jnp.zeros_like(meta)
    for k in range(2):
        meta[k : k + 1, 0:tok] = targets[k]
        meta[k + 2 : k + 3, 0:tok] = scale_ref[k : k + 1, :]
    pl.semaphore_wait(barrier, plane - 1 + 3)

    def leg_one(d, p):
        rows = pl.ds(p * PIECE, PIECE)
        source = tok_ref if d == 0 else cot_ref
        return pltpu.make_async_remote_copy(
            src_ref=source.at[rows], dst_ref=relay.at[d, rows],
            send_sem=s_one.at[d, p], recv_sem=r_one.at[d, p],
            device_id=up if d == 0 else down, device_id_type=MESH,
        )

    def leg_two(d, p):
        rows = pl.ds(p * PIECE, PIECE)
        return pltpu.make_async_remote_copy(
            src_ref=relay.at[d, rows], dst_ref=far.at[d, rows],
            send_sem=s_two.at[d, p], recv_sem=r_two.at[d, p],
            device_id=up if d == 0 else down, device_id_type=MESH,
        )

    meta_copy = pltpu.make_async_remote_copy(
        src_ref=meta, dst_ref=far_meta, send_sem=s_meta, recv_sem=r_meta,
        device_id=across, device_id_type=MESH,
    )
    for p in range(pieces):
        for d in range(2):
            leg_one(d, p).start()
    meta_copy.start()

    def to_plane(s, there):
        rows = pl.multiple_of((s * plane + there) * message, 16)
        into = pl.multiple_of((s * plane + here) * message, 16)
        return pltpu.make_async_remote_copy(
            src_ref=send.at[pl.ds(rows, message)], dst_ref=land.at[pl.ds(into, message)],
            send_sem=s_xy.at[s, there], recv_sem=r_xy.at[s, here],
            device_id=plane_target(lax.div(there, NY), z_hi, lax.rem(there, NY)),
            device_id_type=MESH,
        )

    def to_self(s):
        rows = pl.multiple_of((s * plane + here) * message, 16)
        return pltpu.make_async_copy(
            send.at[pl.ds(rows, message)], land.at[pl.ds(rows, message)], r_xy.at[s, here]
        )

    def from_plane(s, there):
        rows = pl.multiple_of((s * plane + there) * message, 16)
        return pltpu.make_async_remote_copy(
            src_ref=send.at[pl.ds(rows, message)], dst_ref=land.at[pl.ds(rows, message)],
            send_sem=s_xy.at[s, there], recv_sem=r_xy.at[s, there],
            device_id=plane_target(lax.div(there, NY), z_hi, lax.rem(there, NY)),
            device_id_type=MESH,
        )

    pairs = NY // 2
    band = pairs * message

    def build(s, tok_view, cot_view, info):
        for k in range(2):
            scaled[k, ...] = (column_of(info[k + 2 : k + 3, 0:tok]) * cot_view[...].astype(F32)).astype(BF)

        @pl.loop(0, NX)
        def _(step):
            to_x = lax.rem(x + 2 + step, NX)
            for k in range(2):
                base = (to_x * 2 + z_hi) * (NY * capacity) + k * capacity
                want = info[k : k + 1, 0:tok] - base.astype(F32)
                total = None
                for p in range(4):
                    source = tok_view if p < 2 else scaled.at[k]
                    cols = pl.ds((p % 2) * wide, wide)
                    chosen = jnp.where(codes_ref[:, p : p + 1] == want, 1.0, 0.0).astype(BF)
                    term = jnp.dot(chosen, source[:, cols], preferred_element_type=F32)
                    total = term if total is None else total + term
                for yy in range(pairs):
                    rows = (s * plane + to_x * NY + 2 * yy + k) * message
                    send[pl.ds(pl.multiple_of(rows, 16), message), :] = total[
                        yy * message : (yy + 1) * message
                    ].astype(BF)
            for to_y in range(NY):
                there = to_x * NY + to_y

                @pl.when(there != here)
                def _():
                    to_plane(s, there).start()

                @pl.when(there == here)
                def _():
                    to_self(s).start()

    build(0, tok_ref, cot_ref, meta)
    for p in range(pieces):
        for d in range(2):
            leg_one(d, p).wait_recv()
            leg_two(d, p).start()
    meta_copy.wait_recv()
    for p in range(pieces):
        for d in range(2):
            leg_two(d, p).wait_recv()
    build(1, far.at[0], far.at[1], far_meta)

    group = 4 * message
    block = 4 * capacity

    @pl.loop(0, 2 * plane // 4)
    def _(g):
        s = lax.div(g, plane // 4)
        first = lax.rem(g, plane // 4) * 4
        for j in range(4):
            there = first + j

            @pl.when(there != here)
            def _():
                from_plane(s, there).wait_recv()

            @pl.when(there == here)
            def _():
                to_self(s).wait()

        rows = land[pl.ds(pl.multiple_of(g * group, 16), group), :]
        out = jnp.dot(perm_ref[...], rows, preferred_element_type=F32).astype(BF)
        into = pl.ds(pl.multiple_of(g * block, 16), block)
        rows_x_ref[into, 0:wide] = out[0:block]
        rows_x_ref[into, wide:width] = out[block : 2 * block]
        rows_dy_ref[into, 0:wide] = out[2 * block : 3 * block]
        rows_dy_ref[into, wide:width] = out[3 * block : 4 * block]

    for p in range(pieces):
        for d in range(2):
            leg_one(d, p).wait_send()
            leg_two(d, p).wait_send()
    meta_copy.wait_send()

    @pl.loop(1, plane)
    def _(step):
        there = lax.rem(here + step, plane)
        for s in range(2):
            to_plane(s, there).wait_send()


def message_codes():
    pairs = NY // 2
    row = np.arange(pairs * 4 * CAP)
    pair, inside = row // (4 * CAP), row % (4 * CAP)
    part, rank = inside // CAP, inside % CAP
    code = (2 * pair) * CAP + rank
    return np.where(part[:, None] == np.arange(4)[None, :], code[:, None], -1e6).astype(np.float32)


def unfold_order():
    order = np.arange(16 * CAP).reshape(4, 4, CAP).transpose(1, 0, 2).reshape(-1)
    return np.eye(16 * CAP, dtype=np.float32)[order]


def dispatch_call(tokens, cotangent, gate_scale, expert_ids, expert_slots):
    tok, width = tokens.shape
    rows = NX * 2 * NY * CAP
    message = 4 * CAP
    plane = NX * NY
    wide = width // 2
    pieces = tok // PIECE
    dma = pltpu.SemaphoreType.DMA
    return pl.pallas_call(
        dispatch_kernel,
        out_shape=(jax.ShapeDtypeStruct((rows, width), BF),) * 2,
        in_specs=[pl.BlockSpec(memory_space=pltpu.VMEM)] * 7,
        out_specs=[pl.BlockSpec(memory_space=pltpu.VMEM)] * 2,
        scratch_shapes=[
            pltpu.VMEM((2, tok, width), BF),
            pltpu.VMEM((2, tok, width), BF),
            pltpu.VMEM((8, 256), F32),
            pltpu.VMEM((8, 256), F32),
            pltpu.VMEM((2, tok, width), BF),
            pltpu.VMEM((2 * plane * message, wide), BF),
            pltpu.VMEM((2 * plane * message, wide), BF),
            dma((2, pieces)), dma((2, pieces)), dma((2, pieces)), dma((2, pieces)),
            dma, dma, dma((2, plane)), dma((2, plane)),
        ],
        compiler_params=pltpu.CompilerParams(
            collective_id=1, has_side_effects=True, vmem_limit_bytes=40 * 1024 * 1024
        ),
        cost_estimate=pl.CostEstimate(
            flops=4 * rows * tok * width * 4, bytes_accessed=4 * 1024 * 1024, transcendentals=0
        ),
        name="dispatch",
    )(
        tokens, cotangent, gate_scale.T, expert_ids.T, expert_slots,
        jnp.asarray(message_codes()), jnp.asarray(unfold_order(), dtype=BF),
    )


def from_partner(block, axis, stride):
    count = lax.axis_size(axis)
    route = []
    for low in range(count):
        high = low | 1 << stride
        if high != low and high < count:
            route += [(low, high), (high, low)]
    return lax.ppermute(block, axis, route)


def contract_first(left, right):
    return lax.dot_general(
        left, right, (((0,), (0,)), ((), ())), preferred_element_type=jnp.float32
    )


def on_device(
    tokens, cotangent, gate_scale, expert_ids, expert_slots, hot_pairs, w_gate, w_up, w_down
):
    tok_rows, width = tokens.shape
    route_count = expert_ids.shape[1]
    slot_count = lax.axis_size("expert")
    capacity = 2 * tok_rows * route_count // slot_count
    entries = tok_rows * route_count
    expert_iota = jnp.arange(expert_slots.shape[0], dtype=jnp.int32)
    expert_match = expert_ids[:, :, None] == expert_iota
    parity = (jnp.arange(tok_rows, dtype=jnp.int32) % 2)[:, None, None]
    slot_table = jnp.where(parity == 1, expert_slots[:, 1], expert_slots[:, 0])
    route_slot = jnp.sum(jnp.where(expert_match, slot_table, 0), axis=2).reshape(entries)
    slot_hit = (route_slot[:, None] == jnp.arange(slot_count, dtype=jnp.int32)).astype(jnp.int32)
    before = jnp.cumsum(slot_hit, axis=0) - slot_hit
    target = route_slot * capacity + jnp.sum(before * slot_hit, axis=1)
    placing = (
        jnp.arange(slot_count * capacity, dtype=jnp.int32)[:, None] == target[None, :]
    ).astype(jnp.bfloat16)
    rows_x, rows_dy = dispatch_call(tokens, cotangent, gate_scale, expert_ids, expert_slots)
    route_grad, own_grad = expert_call(rows_x, rows_dy, w_gate[0], w_up[0], w_down[0])
    z_hi = lax.axis_index("expert") // NY % 2
    sides = route_grad.reshape(2, NX, NY * CAP, width)
    sides = jnp.where(z_hi == 1, sides[::-1], sides)
    route_grad = jnp.transpose(sides, (1, 0, 2, 3))
    returned = lax.all_to_all(
        route_grad.reshape(slot_count, capacity, width),
        "expert",
        split_axis=0,
        concat_axis=0,
        tiled=True,
    )
    per_route = contract_first(placing, returned.reshape(-1, width))
    grad_tokens = jnp.sum(per_route.reshape(tok_rows, route_count, width), axis=1).astype(
        jnp.bfloat16
    )
    pair_bit = slot_count.bit_length() - 2
    half_slots = slot_count // 2
    hot_flag = jnp.any(hot_pairs == lax.axis_index("expert") % half_slots).astype(jnp.float32)
    partner = from_partner(own_grad.astype(jnp.bfloat16), "expert", pair_bit).astype(own_grad.dtype)
    grad_down = (own_grad + hot_flag * partner).astype(jnp.bfloat16)[None]
    return (grad_tokens, grad_down)


def solution(mesh):
    placed = (
        P("expert", "dp"),
        P("expert", "dp"),
        P("expert", None),
        P("expert", None),
        P(),
        P(),
        P("expert", "dp", None),
        P("expert", "dp", None),
        P("expert", None, "dp"),
    )
    return jax.shard_map(
        on_device,
        mesh=mesh,
        in_specs=placed,
        out_specs=(P("expert", "dp"), P("expert", None, "dp")),
        check_vma=False,
    )
```

```python
import jax
import jax.numpy as jnp
import numpy as np
from jax import lax
from jax.experimental import pallas as pl
from jax.experimental.pallas import tpu as pltpu
from jax.sharding import PartitionSpec as P

BF = jnp.bfloat16
F32 = jnp.float32
MESH = pl.DeviceIdType.MESH
CAP = 12
NX = 4
NY = 8
BLOCK = 256


def swiglu_back(gate_sum, up_sum, grad_hidden):
    sigmoid_gate = jax.nn.sigmoid(gate_sum)
    active = gate_sum * sigmoid_gate
    hidden = (active * up_sum).astype(BF)
    grad_up = (grad_hidden * active).astype(BF)
    grad_gate = (
        grad_hidden * up_sum * sigmoid_gate * (1.0 + gate_sum * (1.0 - sigmoid_gate))
    ).astype(BF)
    return (hidden, grad_gate, grad_up)


def dot_last(left, right):
    return lax.dot_general(left, right, (((1,), (1,)), ((), ())), preferred_element_type=F32)


def dot_first(left, right):
    return lax.dot_general(left, right, (((0,), (0,)), ((), ())), preferred_element_type=F32)


def coords():
    spot = lax.axis_index("expert")
    dp = lax.axis_index("dp")
    y = lax.rem(spot, NY)
    z_hi = lax.rem(lax.div(spot, NY), 2)
    x = lax.div(spot, 2 * NY)
    z_lo = lax.div(dp, 2)
    return x, z_hi, y, z_hi * 4 + z_lo, lax.rem(dp, 2)


def at_place(x, y, z, core):
    return {
        "dp": lax.rem(z, 4) * 2 + core,
        "expert": (x * 2 + lax.div(z, 4)) * NY + y,
    }


def plane_target(x, z_hi, y):
    return {"expert": (x * 2 + z_hi) * NY + y}


def signal_all(barrier, places):
    for place in places:
        pl.semaphore_signal(barrier, inc=1, device_id=place, device_id_type=MESH)


def signal_plane(barrier, x, z_hi, y):
    @pl.loop(1, NX * NY)
    def _(step):
        there = lax.rem(x * NY + y + step, NX * NY)
        pl.semaphore_signal(
            barrier, inc=1,
            device_id=plane_target(lax.div(there, NY), z_hi, lax.rem(there, NY)),
            device_id_type=MESH,
        )


def column_of(row):
    n = row.shape[1]
    diagonal = lax.broadcasted_iota(jnp.int32, (n, n), 0) == lax.broadcasted_iota(
        jnp.int32, (n, n), 1
    )
    return jnp.sum(jnp.where(diagonal, row, 0.0), axis=1, keepdims=True)


def route_targets(ids_ref, slots_ref, slot_count, capacity):
    tok = ids_ref.shape[1]
    experts = slots_ref.shape[0]
    odd = lax.broadcasted_iota(jnp.int32, (experts, tok), 1) % 2 == 1
    table = jnp.where(odd, slots_ref[:, 1:2], slots_ref[:, 0:1])
    expert_row = lax.broadcasted_iota(jnp.int32, (experts, tok), 0)
    slot_row = lax.broadcasted_iota(jnp.int32, (slot_count, tok), 0)
    slots = [
        jnp.sum(jnp.where(ids_ref[k : k + 1, :] == expert_row, table, 0), axis=0, keepdims=True)
        for k in range(2)
    ]
    hits = [jnp.where(slot == slot_row, 1.0, 0.0) for slot in slots]
    earlier = lax.broadcasted_iota(jnp.int32, (tok, tok), 0) < lax.broadcasted_iota(
        jnp.int32, (tok, tok), 1
    )
    before = jnp.dot(
        (hits[0] + hits[1]).astype(BF),
        jnp.where(earlier, 1.0, 0.0).astype(BF),
        preferred_element_type=F32,
    )
    return [
        slot.astype(F32) * capacity + jnp.sum(hit * before, axis=0, keepdims=True)
        for slot, hit in zip(slots, hits)
    ]


def layer_kernel(
    tok_ref, cot_ref, scale_ref, ids_ref, slots_ref, hot_ref, fold_ref, wg_ref, wu_ref, wd_ref,
    grad_tok_ref, grad_down_ref,
    far, meta, far_meta, gather_x, gather_dy, send, land, rows_x, rows_dy,
    part, from_sib, from_prev, done, route, back_send, back_land, returned,
    partial, cross_send, cross_land, own, pair_send, pair_land,
    s_z, r_z, s_meta, r_meta, s_xy, r_xy, s_sib, r_sib, s_rs, r_rs, s_ag, r_ag, s_fin, r_fin,
    s_back, r_back, s_cross, r_cross, s_pair, r_pair,
):
    tok, width = tok_ref.shape
    hid = wg_ref.shape[1]
    blocks = hid // BLOCK
    plane = NX * NY
    side_rows = plane * CAP
    message = 4 * CAP
    group = 4 * message
    wide, thin = width // 2, width // 4
    part_rows = side_rows // 4
    count = 2 * blocks
    x, z_hi, y, z, core = coords()
    here = x * NY + y
    spot = lax.axis_index("expert")
    me = lax.axis_index("dp")
    chip = lax.div(me, 2)
    last = lax.axis_size("dp") // 2 - 1
    sib = {"dp": me + 1 - 2 * core}
    across = at_place(x, y, lax.rem(z + 4, 8), core)
    pair = {"expert": lax.rem(spot + plane, 2 * plane)}
    inner = (chip > 0) & (chip < last)

    barrier = pltpu.get_barrier_semaphore()
    signal_all(barrier, (across, sib))
    signal_plane(barrier, x, z_hi, y)

    @pl.when(chip > 0)
    def _():
        signal_all(barrier, ({"dp": me - 2},))

    @pl.when(chip < last)
    def _():
        signal_all(barrier, ({"dp": me + 2},))

    targets = route_targets(ids_ref, slots_ref, 2 * plane, CAP)
    meta[...] = jnp.zeros_like(meta)
    for k in range(2):
        meta[k : k + 1, 0:tok] = targets[k]
        meta[k + 2 : k + 3, 0:tok] = scale_ref[k : k + 1, :]

    @pl.when(inner)
    def _():
        pl.semaphore_wait(barrier, plane + 3)

    @pl.when(jnp.logical_not(inner))
    def _():
        pl.semaphore_wait(barrier, plane + 2)

    def crossing(d):
        source = tok_ref if d == 0 else cot_ref
        return pltpu.make_async_remote_copy(
            src_ref=source, dst_ref=far.at[d], send_sem=s_z.at[d], recv_sem=r_z.at[d],
            device_id=across, device_id_type=MESH,
        )

    meta_copy = pltpu.make_async_remote_copy(
        src_ref=meta, dst_ref=far_meta, send_sem=s_meta, recv_sem=r_meta,
        device_id=across, device_id_type=MESH,
    )
    meta_copy.start()
    crossing(0).start()
    crossing(1).start()

    def place_rows(s, there):
        return pl.ds(pl.multiple_of((s * plane + there) * message, 16), message)

    def to_plane(source, into, s, there, sent, got):
        return pltpu.make_async_remote_copy(
            src_ref=source.at[place_rows(s, there)], dst_ref=into.at[place_rows(s, here)],
            send_sem=sent.at[s, there], recv_sem=got.at[s, here],
            device_id=plane_target(lax.div(there, NY), z_hi, lax.rem(there, NY)),
            device_id_type=MESH,
        )

    def from_plane(source, into, s, there, sent, got):
        return pltpu.make_async_remote_copy(
            src_ref=source.at[place_rows(s, there)], dst_ref=into.at[place_rows(s, there)],
            send_sem=sent.at[s, there], recv_sem=got.at[s, there],
            device_id=plane_target(lax.div(there, NY), z_hi, lax.rem(there, NY)),
            device_id_type=MESH,
        )

    def to_self(source, into, s, got):
        return pltpu.make_async_copy(
            source.at[place_rows(s, here)], into.at[place_rows(s, here)], got.at[s, here]
        )

    def start_plane(source, into, s, there, sent, got):
        @pl.when(there != here)
        def _():
            to_plane(source, into, s, there, sent, got).start()

        @pl.when(there == here)
        def _():
            to_self(source, into, s, got).start()

    def wait_plane(source, into, s, there, sent, got):
        @pl.when(there != here)
        def _():
            from_plane(source, into, s, there, sent, got).wait_recv()

        @pl.when(there == here)
        def _():
            to_self(source, into, s, got).wait()

    def row_codes(shape, axis):
        row = lax.broadcasted_iota(jnp.int32, shape, axis)
        band = NY * CAP
        code = row + z_hi * band
        for edge in range(1, NX):
            code = code + jnp.where(row >= edge * band, band, 0)
        return code

    def dispatch(s, tok_view, cot_view, info):
        codes = row_codes((side_rows, tok), 0)
        hits = [
            jnp.where(codes == info[k : k + 1, 0:tok].astype(jnp.int32), 1.0, 0.0).astype(BF)
            for k in range(2)
        ]
        gather_x[...] = jnp.dot(
            hits[0] + hits[1], tok_view[...], preferred_element_type=F32
        ).astype(BF)
        cot = cot_view[...].astype(F32)
        scaled = [
            (column_of(info[k + 2 : k + 3, 0:tok]) * cot).astype(BF) for k in range(2)
        ]
        gather_dy[...] = (
            jnp.dot(hits[0], scaled[0], preferred_element_type=F32)
            + jnp.dot(hits[1], scaled[1], preferred_element_type=F32)
        ).astype(BF)

        @pl.loop(0, plane // 4)
        def _(step):
            g = lax.rem(step + 2 * x + plane // 8, plane // 4)
            rows = pl.ds(pl.multiple_of(g * message, 16), message)
            stacked = jnp.concatenate(
                [
                    gather_x[rows, 0:wide], gather_x[rows, wide:width],
                    gather_dy[rows, 0:wide], gather_dy[rows, wide:width],
                ],
                axis=0,
            )
            into = pl.ds(pl.multiple_of((s * plane // 4 + g) * group, 16), group)
            send[into, :] = jnp.dot(
                fold_ref[1], stacked, preferred_element_type=F32
            ).astype(BF)
            for j in range(4):
                start_plane(send, land, s, g * 4 + j, s_xy, r_xy)

    def unfold(s):
        @pl.loop(0, plane // 4)
        def _(g):
            for j in range(4):
                wait_plane(send, land, s, g * 4 + j, s_xy, r_xy)
            here_rows = pl.ds(pl.multiple_of((s * plane // 4 + g) * group, 16), group)
            out = jnp.dot(fold_ref[0], land[here_rows, :], preferred_element_type=F32).astype(BF)
            into = pl.ds(pl.multiple_of((s * plane // 4 + g) * message, 16), message)
            rows_x[into, 0:wide] = out[0:message]
            rows_x[into, wide:width] = out[message : 2 * message]
            rows_dy[into, 0:wide] = out[2 * message : 3 * message]
            rows_dy[into, wide:width] = out[3 * message : 4 * message]

    def own_rows(f, k, which):
        start = lax.div(k, blocks) * side_rows + which * (side_rows // 2) + f * part_rows
        return pl.ds(pl.multiple_of(start, 16), part_rows)

    def buf_rows(f, k):
        start = lax.div(k, blocks) * (side_rows // 2) + f * part_rows
        return pl.ds(pl.multiple_of(start, 16), part_rows)

    def block_of(k):
        return lax.rem(k, blocks)

    def send_sib(f, k):
        return pltpu.make_async_remote_copy(
            src_ref=part.at[block_of(k), own_rows(f, k, 1 - core)],
            dst_ref=from_sib.at[block_of(k), buf_rows(f, k)],
            send_sem=s_sib.at[f, k], recv_sem=r_sib.at[f, k],
            device_id=sib, device_id_type=MESH,
        )

    def send_rs(f, k):
        return pltpu.make_async_remote_copy(
            src_ref=part.at[block_of(k), own_rows(f, k, core)],
            dst_ref=from_prev.at[block_of(k), buf_rows(f, k)],
            send_sem=s_rs.at[f, k], recv_sem=r_rs.at[f, k],
            device_id={"dp": me + 2 if f == 0 else me - 2}, device_id_type=MESH,
        )

    def send_done(f, k, target, sent, got):
        here_done = done.at[block_of(k), own_rows(f, k, core)]
        return pltpu.make_async_remote_copy(
            src_ref=here_done, dst_ref=here_done, send_sem=sent.at[f, k], recv_sem=got.at[f, k],
            device_id=target, device_id_type=MESH,
        )

    def send_ag(f, k):
        return send_done(f, k, {"dp": me - 2 if f == 0 else me + 2}, s_ag, r_ag)

    def send_fin(f, k):
        return send_done(f, k, sib, s_fin, r_fin)

    def parts(side):
        @pl.loop(0, blocks)
        def _(h):
            cols = pl.ds(pl.multiple_of(h * BLOCK, BLOCK), BLOCK)
            for turn in range(2):
                which = 1 - core if turn == 0 else core
                start = pl.multiple_of(side * side_rows + which * (side_rows // 2), 16)
                rows = pl.ds(start, side_rows // 2)
                part[h, rows, 0:BLOCK] = jnp.dot(
                    rows_x[rows, :], wg_ref[:, cols], preferred_element_type=F32
                ).astype(BF)
                part[h, rows, BLOCK : 2 * BLOCK] = jnp.dot(
                    rows_x[rows, :], wu_ref[:, cols], preferred_element_type=F32
                ).astype(BF)
                part[h, rows, 2 * BLOCK : 3 * BLOCK] = dot_last(
                    rows_dy[rows, :], wd_ref[cols, :]
                ).astype(BF)
                if turn == 0:
                    for f in range(2):
                        send_sib(f, side * blocks + h).start()

    def step(tick):
        for f in range(2):
            q = chip if f == 0 else last - chip
            k = tick - q

            @pl.when((k >= 0) & (k < count))
            def _():
                send_sib(f, k).wait_recv()
                mine = own_rows(f, k, core)
                h = block_of(k)
                buf = buf_rows(f, k)

                @pl.when(q == 0)
                def _():
                    part[h, mine, :] = (
                        part[h, mine, :].astype(F32) + from_sib[h, buf, :].astype(F32)
                    ).astype(BF)

                @pl.when(q > 0)
                def _():
                    send_rs(f, k).wait_recv()

                @pl.when((q > 0) & (q < last))
                def _():
                    part[h, mine, :] = (
                        part[h, mine, :].astype(F32)
                        + from_sib[h, buf, :].astype(F32)
                        + from_prev[h, buf, :].astype(F32)
                    ).astype(BF)

                @pl.when(q < last)
                def _():
                    send_rs(f, k).start()

                @pl.when(q == last)
                def _():
                    sums = []
                    for c in range(3):
                        cols = pl.ds(c * BLOCK, BLOCK)
                        sums.append(
                            part[h, mine, cols].astype(F32)
                            + from_sib[h, buf, cols].astype(F32)
                            + from_prev[h, buf, cols].astype(F32)
                        )
                    for c, value in enumerate(swiglu_back(*sums)):
                        done[h, mine, pl.ds(c * BLOCK, BLOCK)] = value
                    send_ag(f, k).start()
                    send_fin(f, k).start()

        for f in range(2):
            q = chip if f == 0 else last - chip
            k = tick - 2 * last + q

            @pl.when((q < last) & (k >= 0) & (k < count))
            def _():
                send_ag(f, k).wait_recv()

                @pl.when(q > 0)
                def _():
                    send_ag(f, k).start()

                send_fin(f, k).start()

    def wait_fin(k):
        for f in range(2):
            send_fin(f, k).wait_recv()

    def send_back(side):
        rows = pl.ds(side * side_rows, side_rows)
        total = None
        for h in range(blocks):
            cols = pl.ds(h * BLOCK, BLOCK)
            term = dot_last(done[h, rows, BLOCK : 2 * BLOCK], wg_ref[:, cols]) + dot_last(
                done[h, rows, 2 * BLOCK : 3 * BLOCK], wu_ref[:, cols]
            )
            total = term if total is None else total + term
        route[...] = total.astype(BF)

        @pl.loop(0, plane // 4)
        def _(g):
            block = pl.ds(pl.multiple_of(g * message, 16), message)
            stacked = jnp.concatenate(
                [route[block, p * thin : (p + 1) * thin] for p in range(4)], axis=0
            )
            into = pl.ds(pl.multiple_of((side * plane // 4 + g) * group, 16), group)
            back_send[into, :] = jnp.dot(
                fold_ref[1], stacked, preferred_element_type=F32
            ).astype(BF)
            for j in range(4):
                start_plane(back_send, back_land, side, g * 4 + j, s_back, r_back)

    def combine(side, info):
        @pl.loop(0, plane // 4)
        def _(g):
            for j in range(4):
                wait_plane(back_send, back_land, side, g * 4 + j, s_back, r_back)
            block = pl.ds(pl.multiple_of((side * plane // 4 + g) * group, 16), group)
            out = jnp.dot(fold_ref[0], back_land[block, :], preferred_element_type=F32).astype(BF)
            into = pl.ds(pl.multiple_of(g * message, 16), message)
            for p in range(4):
                returned[into, p * thin : (p + 1) * thin] = out[p * message : (p + 1) * message]

        codes = row_codes((tok, side_rows), 1)
        hits = None
        for k in range(2):
            hit = codes == column_of(info[k : k + 1, 0:tok]).astype(jnp.int32)
            hits = hit if hits is None else hits | hit
        return jnp.dot(
            jnp.where(hits, 1.0, 0.0).astype(BF), returned[...], preferred_element_type=F32
        )

    dispatch(0, tok_ref, cot_ref, meta)
    meta_copy.wait_recv()
    crossing(0).wait_recv()
    crossing(1).wait_recv()
    dispatch(1, far.at[0], far.at[1], far_meta)

    unfold(0)
    parts(0)
    pl.loop(0, blocks)(step)
    unfold(1)
    parts(1)
    pl.loop(blocks, blocks + 2 * last)(step)

    for k in range(blocks):
        wait_fin(k)
    send_back(0)

    def pair_copy(h):
        rows = pl.ds(pl.multiple_of(h * BLOCK, BLOCK), BLOCK)
        return pltpu.make_async_remote_copy(
            src_ref=pair_send.at[rows], dst_ref=pair_land.at[rows],
            send_sem=s_pair.at[h], recv_sem=r_pair.at[h],
            device_id=pair, device_id_type=MESH,
        )

    @pl.loop(0, blocks)
    def _(h):
        step(h + blocks + 2 * last)
        wait_fin(h + blocks)
        rows = pl.ds(pl.multiple_of(h * BLOCK, BLOCK), BLOCK)
        own[rows, :] = dot_first(done[h, :, 0:BLOCK], rows_dy[...])
        pair_send[rows, :] = own[rows, :].astype(BF)
        pair_copy(h).start()

    send_back(1)

    cross = pltpu.make_async_remote_copy(
        src_ref=cross_send, dst_ref=cross_land, send_sem=s_cross, recv_sem=r_cross,
        device_id=across, device_id_type=MESH,
    )
    partial[...] = combine(0, meta)
    cross_send[...] = combine(1, far_meta).astype(BF)
    cross.start()

    hot = jnp.max(
        jnp.where(hot_ref[...] == lax.rem(spot, plane), 1.0, 0.0), axis=1, keepdims=True
    )

    @pl.loop(0, blocks)
    def _(h):
        pair_copy(h).wait_recv()
        rows = pl.ds(pl.multiple_of(h * BLOCK, BLOCK), BLOCK)
        grad_down_ref[rows, :] = (own[rows, :] + hot * pair_land[rows, :].astype(F32)).astype(BF)

    cross.wait_recv()
    grad_tok_ref[...] = (partial[...] + cross_land[...].astype(F32)).astype(BF)

    meta_copy.wait_send()
    cross.wait_send()
    for d in range(2):
        crossing(d).wait_send()

    @pl.loop(1, plane)
    def _(hop):
        there = lax.rem(here + hop, plane)
        for s in range(2):
            to_plane(send, land, s, there, s_xy, r_xy).wait_send()
            to_plane(back_send, back_land, s, there, s_back, r_back).wait_send()

    @pl.loop(0, count)
    def _(k):
        for f in range(2):
            q = chip if f == 0 else last - chip
            send_sib(f, k).wait_send()
            send_fin(f, k).wait_send()

            @pl.when(q < last)
            def _():
                send_rs(f, k).wait_send()

            @pl.when(q > 0)
            def _():
                send_ag(f, k).wait_send()

    @pl.loop(0, blocks)
    def _(h):
        pair_copy(h).wait_send()


def fold_orders():
    order = np.arange(16 * CAP).reshape(4, 4, CAP).transpose(1, 0, 2).reshape(-1)
    unfold = np.eye(16 * CAP, dtype=np.float32)[order]
    return np.stack([unfold, unfold.T])


def on_device(
    tokens, cotangent, gate_scale, expert_ids, expert_slots, hot_pairs, w_gate, w_up, w_down
):
    tok, width = tokens.shape
    hid = w_gate.shape[2]
    plane = NX * NY
    side_rows = plane * CAP
    rows = 2 * side_rows
    message = 4 * CAP
    blocks = hid // BLOCK
    count = 2 * blocks
    dma = pltpu.SemaphoreType.DMA
    flow = [dma((2, count))] * 8
    grad_tokens, grad_down = pl.pallas_call(
        layer_kernel,
        out_shape=(
            jax.ShapeDtypeStruct((tok, width), BF),
            jax.ShapeDtypeStruct((hid, width), BF),
        ),
        in_specs=[pl.BlockSpec(memory_space=pltpu.VMEM)] * 10,
        out_specs=[pl.BlockSpec(memory_space=pltpu.VMEM)] * 2,
        scratch_shapes=[
            pltpu.VMEM((2, tok, width), BF),
            pltpu.VMEM((8, 256), F32),
            pltpu.VMEM((8, 256), F32),
            pltpu.VMEM((side_rows, width), BF),
            pltpu.VMEM((side_rows, width), BF),
            pltpu.VMEM((2 * plane * message, width // 2), BF),
            pltpu.VMEM((2 * plane * message, width // 2), BF),
            pltpu.VMEM((rows, width), BF),
            pltpu.VMEM((rows, width), BF),
            pltpu.VMEM((blocks, rows, 3 * BLOCK), BF),
            pltpu.VMEM((blocks, side_rows, 3 * BLOCK), BF),
            pltpu.VMEM((blocks, side_rows, 3 * BLOCK), BF),
            pltpu.VMEM((blocks, rows, 3 * BLOCK), BF),
            pltpu.VMEM((side_rows, width), BF),
            pltpu.VMEM((2 * plane * message, width // 4), BF),
            pltpu.VMEM((2 * plane * message, width // 4), BF),
            pltpu.VMEM((side_rows, width), BF),
            pltpu.VMEM((tok, width), F32),
            pltpu.VMEM((tok, width), BF),
            pltpu.VMEM((tok, width), BF),
            pltpu.VMEM((hid, width), F32),
            pltpu.VMEM((hid, width), BF),
            pltpu.VMEM((hid, width), BF),
            dma((2,)), dma((2,)), dma, dma, dma((2, plane)), dma((2, plane)),
        ] + flow + [
            dma((2, plane)), dma((2, plane)), dma, dma, dma((blocks,)), dma((blocks,)),
        ],
        compiler_params=pltpu.CompilerParams(
            collective_id=0, has_side_effects=True, vmem_limit_bytes=52 * 1024 * 1024
        ),
        cost_estimate=pl.CostEstimate(
            flops=12 * rows * width * hid, bytes_accessed=8 * 1024 * 1024, transcendentals=0
        ),
        name="layer_backward",
    )(
        tokens, cotangent, gate_scale.T, expert_ids.T, expert_slots, hot_pairs.reshape(1, -1),
        jnp.asarray(fold_orders(), dtype=BF), w_gate[0], w_up[0], w_down[0],
    )
    return grad_tokens, grad_down[None]


def solution(mesh):
    placed = (
        P("expert", "dp"),
        P("expert", "dp"),
        P("expert", None),
        P("expert", None),
        P(),
        P(),
        P("expert", "dp", None),
        P("expert", "dp", None),
        P("expert", None, "dp"),
    )
    return jax.shard_map(
        on_device,
        mesh=mesh,
        in_specs=placed,
        out_specs=(P("expert", "dp"), P("expert", None, "dp")),
        check_vma=False,
    )
```

```python
import jax
import jax.numpy as jnp
import numpy as np
from jax import lax
from jax.experimental import pallas as pl
from jax.experimental.pallas import tpu as pltpu
from jax.sharding import PartitionSpec as P

BF = jnp.bfloat16
F32 = jnp.float32
MESH = pl.DeviceIdType.MESH
CAP = 12
NX = 4
NY = 8
BLOCK = 256
LAG = 2


def swiglu_back(gate_sum, up_sum, grad_hidden):
    sigmoid_gate = jax.nn.sigmoid(gate_sum)
    active = gate_sum * sigmoid_gate
    hidden = (active * up_sum).astype(BF)
    grad_up = (grad_hidden * active).astype(BF)
    grad_gate = (
        grad_hidden * up_sum * sigmoid_gate * (1.0 + gate_sum * (1.0 - sigmoid_gate))
    ).astype(BF)
    return (hidden, grad_gate, grad_up)


def dot_last(left, right):
    return lax.dot_general(left, right, (((1,), (1,)), ((), ())), preferred_element_type=F32)


def dot_first(left, right):
    return lax.dot_general(left, right, (((0,), (0,)), ((), ())), preferred_element_type=F32)


def coords():
    spot = lax.axis_index("expert")
    dp = lax.axis_index("dp")
    y = lax.rem(spot, NY)
    z_hi = lax.rem(lax.div(spot, NY), 2)
    x = lax.div(spot, 2 * NY)
    z_lo = lax.div(dp, 2)
    return x, z_hi, y, z_hi * 4 + z_lo, lax.rem(dp, 2)


def at_place(x, y, z, core):
    return {
        "dp": lax.rem(z, 4) * 2 + core,
        "expert": (x * 2 + lax.div(z, 4)) * NY + y,
    }


def plane_target(x, z_hi, y):
    return {"expert": (x * 2 + z_hi) * NY + y}


def signal_all(barrier, places):
    for place in places:
        pl.semaphore_signal(barrier, inc=1, device_id=place, device_id_type=MESH)


def signal_plane(barrier, x, z_hi, y):
    @pl.loop(1, NX * NY)
    def _(step):
        there = lax.rem(x * NY + y + step, NX * NY)
        pl.semaphore_signal(
            barrier, inc=1,
            device_id=plane_target(lax.div(there, NY), z_hi, lax.rem(there, NY)),
            device_id_type=MESH,
        )


def column_of(row):
    n = row.shape[1]
    diagonal = lax.broadcasted_iota(jnp.int32, (n, n), 0) == lax.broadcasted_iota(
        jnp.int32, (n, n), 1
    )
    return jnp.sum(jnp.where(diagonal, row, 0.0), axis=1, keepdims=True)


def route_targets(ids_ref, slots_ref, slot_count, capacity):
    tok = ids_ref.shape[1]
    experts = slots_ref.shape[1]
    odd = lax.broadcasted_iota(jnp.int32, (experts, tok), 1) % 2 == 1
    first, second = [column_of(slots_ref[k : k + 1, :].astype(F32)) for k in range(2)]
    table = jnp.where(odd, second, first)
    expert_row = lax.broadcasted_iota(jnp.int32, (experts, tok), 0)
    slot_row = lax.broadcasted_iota(jnp.int32, (slot_count, tok), 0)
    slots = [
        jnp.sum(jnp.where(ids_ref[k : k + 1, :] == expert_row, table, 0.0), axis=0, keepdims=True)
        for k in range(2)
    ]
    hits = [jnp.where(slot.astype(jnp.int32) == slot_row, 1.0, 0.0) for slot in slots]
    earlier = lax.broadcasted_iota(jnp.int32, (tok, tok), 0) < lax.broadcasted_iota(
        jnp.int32, (tok, tok), 1
    )
    before = jnp.dot(
        (hits[0] + hits[1]).astype(BF),
        jnp.where(earlier, 1.0, 0.0).astype(BF),
        preferred_element_type=F32,
    )
    return [
        slot * capacity + jnp.sum(hit * before, axis=0, keepdims=True)
        for slot, hit in zip(slots, hits)
    ]


def layer_kernel(
    tok_any, cot_any, scale_any, ids_any, slots_any, hot_any, fold_any, wg_any, wu_any, wd_any,
    grad_tok_ref, grad_down_ref,
    ids_ref, slots_ref, scale_ref, tok_ref, cot_ref, fold_ref, hot_ref, wg_ref, wu_ref, wd_ref,
    far, meta, far_meta, gather_x, gather_dy, send, land, rows_x, rows_dy,
    part, from_sib, from_prev, done, route, back_send, back_land, returned,
    partial, cross_send, cross_land, own, hid_send, pair_hid, pair_dy,
    s_z, r_z, s_meta, r_meta, s_xy, r_xy, s_sib, r_sib, s_rs, r_rs, s_ag, r_ag, s_fin, r_fin,
    s_back, r_back, s_cross, r_cross, s_pair, r_pair, s_pdy, r_pdy, s_half, r_half, s_load,
):
    tok, width = tok_ref.shape
    hid = wg_ref.shape[1]
    blocks = hid // BLOCK
    plane = NX * NY
    side_rows = plane * CAP
    message = 4 * CAP
    group = 4 * message
    wide, thin = width // 2, width // 4
    stage_rows = side_rows // 2
    part_rows = stage_rows // 4
    count = 4 * blocks
    x, z_hi, y, z, core = coords()
    here = x * NY + y
    spot = lax.axis_index("expert")
    me = lax.axis_index("dp")
    chip = lax.div(me, 2)
    last = lax.axis_size("dp") // 2 - 1
    sib = {"dp": me + 1 - 2 * core}
    across = at_place(x, y, lax.rem(z + 4, 8), core)
    pair = {"expert": lax.rem(spot + plane, 2 * plane)}
    inner = (chip > 0) & (chip < last)

    held = [
        (ids_any, ids_ref), (slots_any, slots_ref), (scale_any, scale_ref), (tok_any, tok_ref),
        (cot_any, cot_ref), (fold_any, fold_ref), (hot_any, hot_ref),
        (wg_any, wg_ref), (wu_any, wu_ref), (wd_any, wd_ref),
    ]
    loads = [
        pltpu.make_async_copy(there, kept, s_load.at[i]) for i, (there, kept) in enumerate(held)
    ]
    for load in loads:
        load.start()

    barrier = pltpu.get_barrier_semaphore()
    signal_all(barrier, (across, sib))
    signal_plane(barrier, x, z_hi, y)

    @pl.when(chip > 0)
    def _():
        signal_all(barrier, ({"dp": me - 2},))

    @pl.when(chip < last)
    def _():
        signal_all(barrier, ({"dp": me + 2},))

    for load in loads[:3]:
        load.wait()
    targets = route_targets(ids_ref, slots_ref, 2 * plane, CAP)
    meta[...] = jnp.zeros_like(meta)
    for k in range(2):
        meta[k : k + 1, 0:tok] = targets[k]
        meta[k + 2 : k + 3, 0:tok] = scale_ref[k : k + 1, :]

    @pl.when(inner)
    def _():
        pl.semaphore_wait(barrier, plane + 3)

    @pl.when(jnp.logical_not(inner))
    def _():
        pl.semaphore_wait(barrier, plane + 2)

    def crossing(d):
        source = tok_any if d == 0 else cot_any
        return pltpu.make_async_remote_copy(
            src_ref=source, dst_ref=far.at[d], send_sem=s_z.at[d], recv_sem=r_z.at[d],
            device_id=across, device_id_type=MESH,
        )

    meta_copy = pltpu.make_async_remote_copy(
        src_ref=meta, dst_ref=far_meta, send_sem=s_meta, recv_sem=r_meta,
        device_id=across, device_id_type=MESH,
    )
    meta_copy.start()
    crossing(0).start()
    crossing(1).start()

    def place_rows(s, there):
        return pl.ds(pl.multiple_of((s * plane + there) * message, 16), message)

    def to_plane(source, into, s, there, sent, got):
        return pltpu.make_async_remote_copy(
            src_ref=source.at[place_rows(s, there)], dst_ref=into.at[place_rows(s, here)],
            send_sem=sent.at[s, there], recv_sem=got.at[s, here],
            device_id=plane_target(lax.div(there, NY), z_hi, lax.rem(there, NY)),
            device_id_type=MESH,
        )

    def from_plane(source, into, s, there, sent, got):
        return pltpu.make_async_remote_copy(
            src_ref=source.at[place_rows(s, there)], dst_ref=into.at[place_rows(s, there)],
            send_sem=sent.at[s, there], recv_sem=got.at[s, there],
            device_id=plane_target(lax.div(there, NY), z_hi, lax.rem(there, NY)),
            device_id_type=MESH,
        )

    def to_self(source, into, s, got):
        return pltpu.make_async_copy(
            source.at[place_rows(s, here)], into.at[place_rows(s, here)], got.at[s, here]
        )

    def start_plane(source, into, s, there, sent, got):
        @pl.when(there != here)
        def _():
            to_plane(source, into, s, there, sent, got).start()

        @pl.when(there == here)
        def _():
            to_self(source, into, s, got).start()

    def wait_plane(source, into, s, there, sent, got):
        @pl.when(there != here)
        def _():
            from_plane(source, into, s, there, sent, got).wait_recv()

        @pl.when(there == here)
        def _():
            to_self(source, into, s, got).wait()

    def row_codes(shape, axis):
        row = lax.broadcasted_iota(jnp.int32, shape, axis)
        band = NY * CAP
        code = row + z_hi * band
        for edge in range(1, NX):
            code = code + jnp.where(row >= edge * band, band, 0)
        return code

    def dispatch(s, tok_view, cot_view, info):
        codes = row_codes((side_rows, tok), 0)
        hits = [
            jnp.where(codes == info[k : k + 1, 0:tok].astype(jnp.int32), 1.0, 0.0).astype(BF)
            for k in range(2)
        ]
        gather_x[...] = jnp.dot(
            hits[0] + hits[1], tok_view[...], preferred_element_type=F32
        ).astype(BF)
        cot = cot_view[...].astype(F32)
        scaled = [
            (column_of(info[k + 2 : k + 3, 0:tok]) * cot).astype(BF) for k in range(2)
        ]
        gather_dy[...] = (
            jnp.dot(hits[0], scaled[0], preferred_element_type=F32)
            + jnp.dot(hits[1], scaled[1], preferred_element_type=F32)
        ).astype(BF)

        @pl.loop(0, plane // 4)
        def _(step):
            g = lax.rem(step + 2 * x, plane // 4)
            rows = pl.ds(pl.multiple_of(g * message, 16), message)
            stacked = jnp.concatenate(
                [
                    gather_x[rows, 0:wide], gather_x[rows, wide:width],
                    gather_dy[rows, 0:wide], gather_dy[rows, wide:width],
                ],
                axis=0,
            )
            into = pl.ds(pl.multiple_of((s * plane // 4 + g) * group, 16), group)
            send[into, :] = jnp.dot(
                fold_ref[1], stacked, preferred_element_type=F32
            ).astype(BF)
            for j in range(4):
                start_plane(send, land, s, g * 4 + j, s_xy, r_xy)

    def group_at(spot_at):
        column = lax.rem(x + NX - lax.div(spot_at, 2), NX)
        return column * 2 + lax.rem(spot_at, 2)

    def unfold(stage):
        s = stage // 2

        @pl.loop(0, plane // 8)
        def _(i):
            spot_at = (stage % 2) * (plane // 8) + i
            g = group_at(spot_at)
            for j in range(4):
                wait_plane(send, land, s, g * 4 + j, s_xy, r_xy)
            here_rows = pl.ds(pl.multiple_of((s * plane // 4 + g) * group, 16), group)
            out = jnp.dot(fold_ref[0], land[here_rows, :], preferred_element_type=F32).astype(BF)
            into = pl.ds(pl.multiple_of((s * plane // 4 + spot_at) * message, 16), message)
            rows_x[into, 0:wide] = out[0:message]
            rows_x[into, wide:width] = out[message : 2 * message]
            rows_dy[into, 0:wide] = out[2 * message : 3 * message]
            rows_dy[into, wide:width] = out[3 * message : 4 * message]

    def own_rows(f, k, which):
        start = lax.div(k, blocks) * stage_rows + which * (stage_rows // 2) + f * part_rows
        return pl.ds(pl.multiple_of(start, 16), part_rows)

    def buf_rows(f, k):
        start = lax.div(k, blocks) * (stage_rows // 2) + f * part_rows
        return pl.ds(pl.multiple_of(start, 16), part_rows)

    def block_of(k):
        return lax.rem(k, blocks)

    def send_sib(f, k):
        return pltpu.make_async_remote_copy(
            src_ref=part.at[block_of(k), own_rows(f, k, 1 - core)],
            dst_ref=from_sib.at[block_of(k), buf_rows(f, k)],
            send_sem=s_sib.at[f, k], recv_sem=r_sib.at[f, k],
            device_id=sib, device_id_type=MESH,
        )

    def send_rs(f, k):
        return pltpu.make_async_remote_copy(
            src_ref=part.at[block_of(k), own_rows(f, k, core)],
            dst_ref=from_prev.at[block_of(k), buf_rows(f, k)],
            send_sem=s_rs.at[f, k], recv_sem=r_rs.at[f, k],
            device_id={"dp": me + 2 if f == 0 else me - 2}, device_id_type=MESH,
        )

    def send_done(f, k, target, sent, got):
        here_done = done.at[block_of(k), own_rows(f, k, core)]
        return pltpu.make_async_remote_copy(
            src_ref=here_done, dst_ref=here_done, send_sem=sent.at[f, k], recv_sem=got.at[f, k],
            device_id=target, device_id_type=MESH,
        )

    def send_ag(f, k):
        return send_done(f, k, {"dp": me - 2 if f == 0 else me + 2}, s_ag, r_ag)

    def send_fin(f, k):
        return send_done(f, k, sib, s_fin, r_fin)

    def parts(stage, h):
        rows = pl.ds(stage * stage_rows, stage_rows)
        cols = pl.ds(pl.multiple_of(h * BLOCK, BLOCK), BLOCK)
        part[h, rows, 0:BLOCK] = jnp.dot(
            rows_x[rows, :], wg_ref[:, cols], preferred_element_type=F32
        ).astype(BF)
        part[h, rows, BLOCK : 2 * BLOCK] = jnp.dot(
            rows_x[rows, :], wu_ref[:, cols], preferred_element_type=F32
        ).astype(BF)
        part[h, rows, 2 * BLOCK : 3 * BLOCK] = dot_last(rows_dy[rows, :], wd_ref[cols, :]).astype(BF)
        for f in range(2):
            send_sib(f, stage * blocks + h).start()

    def step(tick):
        for f in range(2):
            q = chip if f == 0 else last - chip
            k = tick - 1 - LAG * q

            @pl.when((k >= 0) & (k < count))
            def _():
                send_sib(f, k).wait_recv()
                mine = own_rows(f, k, core)
                h = block_of(k)
                buf = buf_rows(f, k)

                @pl.when(q == 0)
                def _():
                    part[h, mine, :] = (
                        part[h, mine, :].astype(F32) + from_sib[h, buf, :].astype(F32)
                    ).astype(BF)

                @pl.when(q > 0)
                def _():
                    send_rs(f, k).wait_recv()

                @pl.when((q > 0) & (q < last))
                def _():
                    part[h, mine, :] = (
                        part[h, mine, :].astype(F32)
                        + from_sib[h, buf, :].astype(F32)
                        + from_prev[h, buf, :].astype(F32)
                    ).astype(BF)

                @pl.when(q < last)
                def _():
                    send_rs(f, k).start()

                @pl.when(q == last)
                def _():
                    sums = []
                    for c in range(3):
                        cols = pl.ds(c * BLOCK, BLOCK)
                        sums.append(
                            part[h, mine, cols].astype(F32)
                            + from_sib[h, buf, cols].astype(F32)
                            + from_prev[h, buf, cols].astype(F32)
                        )
                    for c, value in enumerate(swiglu_back(*sums)):
                        done[h, mine, pl.ds(c * BLOCK, BLOCK)] = value
                    send_ag(f, k).start()
                    send_fin(f, k).start()

        for f in range(2):
            q = chip if f == 0 else last - chip
            k = tick - 1 - LAG * (2 * last - q)

            @pl.when((q < last) & (k >= 0) & (k < count))
            def _():
                send_ag(f, k).wait_recv()

                @pl.when(q > 0)
                def _():
                    send_ag(f, k).start()

                send_fin(f, k).start()

    def wait_fin(k):
        for f in range(2):
            send_fin(f, k).wait_recv()

    def send_back(stage):
        side = stage // 2
        rows = pl.ds(stage * stage_rows, stage_rows)
        total = None
        for h in range(blocks):
            cols = pl.ds(h * BLOCK, BLOCK)
            term = dot_last(done[h, rows, BLOCK : 2 * BLOCK], wg_ref[:, cols]) + dot_last(
                done[h, rows, 2 * BLOCK : 3 * BLOCK], wu_ref[:, cols]
            )
            total = term if total is None else total + term
        route[...] = total.astype(BF)

        @pl.loop(0, plane // 8)
        def _(i):
            g = group_at((stage % 2) * (plane // 8) + i)
            block = pl.ds(pl.multiple_of(i * message, 16), message)
            stacked = jnp.concatenate(
                [route[block, p * thin : (p + 1) * thin] for p in range(4)], axis=0
            )
            into = pl.ds(pl.multiple_of((side * plane // 4 + g) * group, 16), group)
            back_send[into, :] = jnp.dot(
                fold_ref[1], stacked, preferred_element_type=F32
            ).astype(BF)
            for j in range(4):
                start_plane(back_send, back_land, side, g * 4 + j, s_back, r_back)

    def combine(side, info):
        @pl.loop(0, plane // 4)
        def _(g):
            for j in range(4):
                wait_plane(back_send, back_land, side, g * 4 + j, s_back, r_back)
            block = pl.ds(pl.multiple_of((side * plane // 4 + g) * group, 16), group)
            out = jnp.dot(fold_ref[0], back_land[block, :], preferred_element_type=F32).astype(BF)
            into = pl.ds(pl.multiple_of(g * message, 16), message)
            for p in range(4):
                returned[into, p * thin : (p + 1) * thin] = out[p * message : (p + 1) * message]

        codes = row_codes((tok, side_rows), 1)
        hits = None
        for k in range(2):
            hit = codes == column_of(info[k : k + 1, 0:tok]).astype(jnp.int32)
            hits = hit if hits is None else hits | hit
        return jnp.dot(
            jnp.where(hits, 1.0, 0.0).astype(BF), returned[...], preferred_element_type=F32
        )

    for load in loads[3:7]:
        load.wait()
    dispatch(0, tok_ref, cot_ref, meta)
    meta_copy.wait_recv()
    crossing(0).wait_recv()
    crossing(1).wait_recv()
    dispatch(1, far.at[0], far.at[1], far_meta)

    def pair_dy_copy(stage):
        rows = pl.ds(stage * stage_rows, stage_rows)
        return pltpu.make_async_remote_copy(
            src_ref=rows_dy.at[rows], dst_ref=pair_dy.at[rows],
            send_sem=s_pdy.at[stage], recv_sem=r_pdy.at[stage],
            device_id=pair, device_id_type=MESH,
        )

    half_rows = stage_rows // 2

    def core_half(stage):
        return pl.ds(pl.multiple_of(stage * stage_rows + core * half_rows, 16), half_rows)

    def pair_hid_copy(stage):
        return pltpu.make_async_remote_copy(
            src_ref=hid_send.at[pl.ds(stage * half_rows, half_rows)],
            dst_ref=pair_hid.at[core_half(stage)],
            send_sem=s_pair.at[stage], recv_sem=r_pair.at[stage],
            device_id=pair, device_id_type=MESH,
        )

    def share_half(stage):
        return pltpu.make_async_remote_copy(
            src_ref=pair_hid.at[core_half(stage)], dst_ref=pair_hid.at[core_half(stage)],
            send_sem=s_half.at[stage], recv_sem=r_half.at[stage],
            device_id=sib, device_id_type=MESH,
        )

    def send_hidden(stage):
        for h in range(blocks):
            hid_send[pl.ds(stage * half_rows, half_rows), pl.ds(h * BLOCK, BLOCK)] = done[
                h, core_half(stage), 0:BLOCK
            ]
        pair_hid_copy(stage).start()

    def pass_on(stage):
        pair_hid_copy(stage).wait_recv()
        share_half(stage).start()

    for load in loads[7:]:
        load.wait()
    drain = 1 + 2 * LAG * last
    stages = count // blocks

    def finish(stage):
        for h in range(blocks):
            wait_fin(stage * blocks + h)
        send_hidden(stage)
        send_back(stage)
        if stage > 0:
            pass_on(stage - 1)

    finished = 0
    tick = 0
    for stage in range(stages):
        unfold(stage)
        pair_dy_copy(stage).start()

        @pl.loop(0, blocks)
        def _(h):
            parts(stage, h)
            step(stage * blocks + h)

        tick += blocks
    while finished < stages - 1:
        stop = (finished + 1) * blocks + drain
        pl.loop(tick, stop)(step)
        tick = stop
        finish(finished)
        finished += 1

    pl.loop(tick, tick + blocks)(step)
    finish(stages - 1)

    @pl.loop(0, blocks)
    def _(h):
        rows = pl.ds(pl.multiple_of(h * BLOCK, BLOCK), BLOCK)
        own[rows, :] = dot_first(done[h, :, 0:BLOCK], rows_dy[...])

    cross = pltpu.make_async_remote_copy(
        src_ref=cross_send, dst_ref=cross_land, send_sem=s_cross, recv_sem=r_cross,
        device_id=across, device_id_type=MESH,
    )
    partial[...] = combine(0, meta)
    pass_on(stages - 1)
    cross_send[...] = combine(1, far_meta).astype(BF)
    cross.start()

    hot = jnp.max(
        jnp.where(hot_ref[...] == lax.rem(spot, plane), 1.0, 0.0), axis=1, keepdims=True
    )

    for stage in range(stages):
        pair_dy_copy(stage).wait_recv()
        share_half(stage).wait_recv()

    @pl.loop(0, blocks)
    def _(h):
        rows = pl.ds(pl.multiple_of(h * BLOCK, BLOCK), BLOCK)
        theirs = dot_first(pair_hid[:, rows], pair_dy[...])
        grad_down_ref[rows, :] = (own[rows, :] + hot * theirs).astype(BF)

    cross.wait_recv()
    grad_tok_ref[...] = (partial[...] + cross_land[...].astype(F32)).astype(BF)

    meta_copy.wait_send()
    cross.wait_send()
    for d in range(2):
        crossing(d).wait_send()

    @pl.loop(1, plane)
    def _(hop):
        there = lax.rem(here + hop, plane)
        for s in range(2):
            to_plane(send, land, s, there, s_xy, r_xy).wait_send()
            to_plane(back_send, back_land, s, there, s_back, r_back).wait_send()

    @pl.loop(0, count)
    def _(k):
        for f in range(2):
            q = chip if f == 0 else last - chip
            send_sib(f, k).wait_send()
            send_fin(f, k).wait_send()

            @pl.when(q < last)
            def _():
                send_rs(f, k).wait_send()

            @pl.when(q > 0)
            def _():
                send_ag(f, k).wait_send()

    for stage in range(stages):
        pair_dy_copy(stage).wait_send()
        pair_hid_copy(stage).wait_send()
        share_half(stage).wait_send()


def fold_orders():
    order = np.arange(16 * CAP).reshape(4, 4, CAP).transpose(1, 0, 2).reshape(-1)
    unfold = np.eye(16 * CAP, dtype=np.float32)[order]
    return np.stack([unfold, unfold.T])


def on_device(
    tokens, cotangent, gate_scale, expert_ids, expert_slots, hot_pairs, w_gate, w_up, w_down
):
    tok, width = tokens.shape
    hid = w_gate.shape[2]
    plane = NX * NY
    side_rows = plane * CAP
    rows = 2 * side_rows
    message = 4 * CAP
    blocks = hid // BLOCK
    count = 4 * blocks
    dma = pltpu.SemaphoreType.DMA
    flow = [dma((2, count))] * 8
    grad_tokens, grad_down = pl.pallas_call(
        layer_kernel,
        out_shape=(
            jax.ShapeDtypeStruct((tok, width), BF),
            jax.ShapeDtypeStruct((hid, width), BF),
        ),
        in_specs=[pl.BlockSpec(memory_space=pl.ANY)] * 10,
        out_specs=[pl.BlockSpec(memory_space=pltpu.VMEM)] * 2,
        scratch_shapes=[
            pltpu.VMEM(expert_ids.shape[::-1], jnp.int32),
            pltpu.VMEM(expert_slots.shape[::-1], jnp.int32),
            pltpu.VMEM(gate_scale.shape[::-1], F32),
            pltpu.VMEM((tok, width), BF),
            pltpu.VMEM((tok, width), BF),
            pltpu.VMEM((2, 16 * CAP, 16 * CAP), BF),
            pltpu.VMEM((1, hot_pairs.shape[0]), jnp.int32),
            pltpu.VMEM((width, hid), BF),
            pltpu.VMEM((width, hid), BF),
            pltpu.VMEM((hid, width), BF),
            pltpu.VMEM((2, tok, width), BF),
            pltpu.VMEM((8, 256), F32),
            pltpu.VMEM((8, 256), F32),
            pltpu.VMEM((side_rows, width), BF),
            pltpu.VMEM((side_rows, width), BF),
            pltpu.VMEM((2 * plane * message, width // 2), BF),
            pltpu.VMEM((2 * plane * message, width // 2), BF),
            pltpu.VMEM((rows, width), BF),
            pltpu.VMEM((rows, width), BF),
            pltpu.VMEM((blocks, rows, 3 * BLOCK), BF),
            pltpu.VMEM((blocks, side_rows, 3 * BLOCK), BF),
            pltpu.VMEM((blocks, side_rows, 3 * BLOCK), BF),
            pltpu.VMEM((blocks, rows, 3 * BLOCK), BF),
            pltpu.VMEM((side_rows // 2, width), BF),
            pltpu.VMEM((2 * plane * message, width // 4), BF),
            pltpu.VMEM((2 * plane * message, width // 4), BF),
            pltpu.VMEM((side_rows, width), BF),
            pltpu.VMEM((tok, width), F32),
            pltpu.VMEM((tok, width), BF),
            pltpu.VMEM((tok, width), BF),
            pltpu.VMEM((hid, width), F32),
            pltpu.VMEM((side_rows, hid), BF),
            pltpu.VMEM((rows, hid), BF),
            pltpu.VMEM((rows, width), BF),
            dma((2,)), dma((2,)), dma, dma, dma((2, plane)), dma((2, plane)),
        ] + flow + [
            dma((2, plane)), dma((2, plane)), dma, dma, dma((4,)), dma((4,)),
            dma((4,)), dma((4,)), dma((4,)), dma((4,)), dma((10,)),
        ],
        compiler_params=pltpu.CompilerParams(
            collective_id=0, has_side_effects=True, vmem_limit_bytes=52 * 1024 * 1024
        ),
        cost_estimate=pl.CostEstimate(
            flops=12 * rows * width * hid, bytes_accessed=8 * 1024 * 1024, transcendentals=0
        ),
        name="layer_backward",
    )(
        tokens, cotangent, gate_scale.T, expert_ids.T, expert_slots.T, hot_pairs.reshape(1, -1),
        jnp.asarray(fold_orders(), dtype=BF), w_gate[0], w_up[0], w_down[0],
    )
    return grad_tokens, grad_down[None]


def solution(mesh):
    placed = (
        P("expert", "dp"),
        P("expert", "dp"),
        P("expert", None),
        P("expert", None),
        P(),
        P(),
        P("expert", "dp", None),
        P("expert", "dp", None),
        P("expert", None, "dp"),
    )
    return jax.shard_map(
        on_device,
        mesh=mesh,
        in_specs=placed,
        out_specs=(P("expert", "dp"), P("expert", None, "dp")),
        check_vma=False,
    )
```

```python
import jax
import jax.numpy as jnp
from jax import lax
from jax.experimental import pallas as pl
from jax.experimental.pallas import tpu as pltpu
from jax.sharding import PartitionSpec as P

BF = jnp.bfloat16
F32 = jnp.float32
MESH = pl.DeviceIdType.MESH
CAP = 12
NX = 4
NY = 8
BLOCK = 256
LAG = 2


def swiglu_back(gate_sum, up_sum, grad_hidden):
    sigmoid_gate = jax.nn.sigmoid(gate_sum)
    active = gate_sum * sigmoid_gate
    hidden = (active * up_sum).astype(BF)
    grad_up = (grad_hidden * active).astype(BF)
    grad_gate = (
        grad_hidden * up_sum * sigmoid_gate * (1.0 + gate_sum * (1.0 - sigmoid_gate))
    ).astype(BF)
    return (hidden, grad_gate, grad_up)


def dot_last(left, right):
    return lax.dot_general(left, right, (((1,), (1,)), ((), ())), preferred_element_type=F32)


def dot_first(left, right):
    return lax.dot_general(left, right, (((0,), (0,)), ((), ())), preferred_element_type=F32)


def coords():
    spot = lax.axis_index("expert")
    dp = lax.axis_index("dp")
    y = lax.rem(spot, NY)
    z_hi = lax.rem(lax.div(spot, NY), 2)
    x = lax.div(spot, 2 * NY)
    z_lo = lax.div(dp, 2)
    return x, z_hi, y, z_hi * 4 + z_lo, lax.rem(dp, 2)


def at_place(x, y, z, core):
    return {
        "dp": lax.rem(z, 4) * 2 + core,
        "expert": (x * 2 + lax.div(z, 4)) * NY + y,
    }


def plane_target(x, z_hi, y):
    return {"expert": (x * 2 + z_hi) * NY + y}


def signal_all(barrier, places):
    for place in places:
        pl.semaphore_signal(barrier, inc=1, device_id=place, device_id_type=MESH)


def signal_plane(barrier, x, z_hi, y):
    @pl.loop(1, NX * NY)
    def _(step):
        there = lax.rem(x * NY + y + step, NX * NY)
        pl.semaphore_signal(
            barrier, inc=1,
            device_id=plane_target(lax.div(there, NY), z_hi, lax.rem(there, NY)),
            device_id_type=MESH,
        )


def column_of(row):
    n = row.shape[1]
    diagonal = lax.broadcasted_iota(jnp.int32, (n, n), 0) == lax.broadcasted_iota(
        jnp.int32, (n, n), 1
    )
    return jnp.sum(jnp.where(diagonal, row, 0.0), axis=1, keepdims=True)


def route_targets(ids_ref, slots_ref, slot_count, capacity):
    tok = ids_ref.shape[1]
    experts = slots_ref.shape[1]
    odd = lax.broadcasted_iota(jnp.int32, (experts, tok), 1) % 2 == 1
    first, second = [column_of(slots_ref[k : k + 1, :].astype(F32)) for k in range(2)]
    table = jnp.where(odd, second, first)
    expert_row = lax.broadcasted_iota(jnp.int32, (experts, tok), 0)
    slot_row = lax.broadcasted_iota(jnp.int32, (slot_count, tok), 0)
    slots = [
        jnp.sum(jnp.where(ids_ref[k : k + 1, :] == expert_row, table, 0.0), axis=0, keepdims=True)
        for k in range(2)
    ]
    hits = [jnp.where(slot.astype(jnp.int32) == slot_row, 1.0, 0.0) for slot in slots]
    earlier = lax.broadcasted_iota(jnp.int32, (tok, tok), 0) < lax.broadcasted_iota(
        jnp.int32, (tok, tok), 1
    )
    before = jnp.dot(
        (hits[0] + hits[1]).astype(BF),
        jnp.where(earlier, 1.0, 0.0).astype(BF),
        preferred_element_type=F32,
    )
    return [
        slot * capacity + jnp.sum(hit * before, axis=0, keepdims=True)
        for slot, hit in zip(slots, hits)
    ]


def fold_matrices(fold_ref):
    size = fold_ref.shape[1]
    message = size // 4
    both = []
    for axis in range(2):
        row = lax.broadcasted_iota(jnp.int32, (size, size), axis)
        outer = sum(jnp.where(row >= e * message, 1, 0) for e in range(1, 4))
        rest = row - outer * message
        inner = sum(jnp.where(rest >= e * CAP, 1, 0) for e in range(1, 4))
        both.append(inner * message + outer * CAP + rest - inner * CAP)
    other = [lax.broadcasted_iota(jnp.int32, (size, size), 1 - axis) for axis in range(2)]
    for axis in range(2):
        fold_ref[axis, :, :] = jnp.where(both[axis] == other[axis], 1.0, 0.0).astype(BF)


def layer_kernel(
    tok_any, cot_any, scale_any, ids_any, slots_any, hot_any, wg_any, wu_any, wd_any,
    grad_tok_ref, grad_down_ref,
    ids_ref, slots_ref, scale_ref, tok_ref, cot_ref, hot_ref, fold_ref, wg_ref, wu_ref, wd_ref,
    far, meta, far_meta, gather_x, gather_dy, send, land, rows_x, rows_dy,
    part, from_sib, from_prev, done, route, back_send, back_land, returned,
    partial, cross_send, cross_land, own, hid_send, pair_hid, pair_dy,
    s_z, r_z, s_meta, r_meta, s_xy, r_xy, s_sib, r_sib, s_rs, r_rs, s_ag, r_ag, s_fin, r_fin,
    s_back, r_back, s_cross, r_cross, s_pair, r_pair, s_pdy, r_pdy, s_half, r_half, s_load,
):
    tok, width = tok_ref.shape
    hid = wg_ref.shape[1]
    blocks = hid // BLOCK
    plane = NX * NY
    side_rows = plane * CAP
    message = 4 * CAP
    group = 4 * message
    wide, thin = width // 2, width // 4
    stage_rows = side_rows // 2
    part_rows = stage_rows // 4
    count = 4 * blocks
    x, z_hi, y, z, core = coords()
    here = x * NY + y
    spot = lax.axis_index("expert")
    me = lax.axis_index("dp")
    chip = lax.div(me, 2)
    last = lax.axis_size("dp") // 2 - 1
    sib = {"dp": me + 1 - 2 * core}
    across = at_place(x, y, lax.rem(z + 4, 8), core)
    pair = {"expert": lax.rem(spot + plane, 2 * plane)}
    inner = (chip > 0) & (chip < last)

    held = [
        (ids_any, ids_ref), (slots_any, slots_ref), (scale_any, scale_ref), (tok_any, tok_ref),
        (cot_any, cot_ref), (hot_any, hot_ref),
        (wg_any, wg_ref), (wu_any, wu_ref), (wd_any, wd_ref),
    ]
    loads = [
        pltpu.make_async_copy(there, kept, s_load.at[i]) for i, (there, kept) in enumerate(held)
    ]
    for load in loads:
        load.start()

    barrier = pltpu.get_barrier_semaphore()
    signal_all(barrier, (across, sib))
    signal_plane(barrier, x, z_hi, y)

    @pl.when(chip > 0)
    def _():
        signal_all(barrier, ({"dp": me - 2},))

    @pl.when(chip < last)
    def _():
        signal_all(barrier, ({"dp": me + 2},))

    fold_matrices(fold_ref)
    for load in loads[:3]:
        load.wait()
    targets = route_targets(ids_ref, slots_ref, 2 * plane, CAP)
    meta[...] = jnp.zeros_like(meta)
    for k in range(2):
        meta[k : k + 1, 0:tok] = targets[k]
        meta[k + 2 : k + 3, 0:tok] = scale_ref[k : k + 1, :]

    @pl.when(inner)
    def _():
        pl.semaphore_wait(barrier, plane + 3)

    @pl.when(jnp.logical_not(inner))
    def _():
        pl.semaphore_wait(barrier, plane + 2)

    def crossing(d):
        source = tok_any if d == 0 else cot_any
        return pltpu.make_async_remote_copy(
            src_ref=source, dst_ref=far.at[d], send_sem=s_z.at[d], recv_sem=r_z.at[d],
            device_id=across, device_id_type=MESH,
        )

    meta_copy = pltpu.make_async_remote_copy(
        src_ref=meta, dst_ref=far_meta, send_sem=s_meta, recv_sem=r_meta,
        device_id=across, device_id_type=MESH,
    )
    meta_copy.start()
    crossing(0).start()
    crossing(1).start()

    def place_rows(s, there):
        return pl.ds(pl.multiple_of((s * plane + there) * message, 16), message)

    def to_plane(source, into, s, there, sent, got):
        return pltpu.make_async_remote_copy(
            src_ref=source.at[place_rows(s, there)], dst_ref=into.at[place_rows(s, here)],
            send_sem=sent.at[s, there], recv_sem=got.at[s, here],
            device_id=plane_target(lax.div(there, NY), z_hi, lax.rem(there, NY)),
            device_id_type=MESH,
        )

    def from_plane(source, into, s, there, sent, got):
        return pltpu.make_async_remote_copy(
            src_ref=source.at[place_rows(s, there)], dst_ref=into.at[place_rows(s, there)],
            send_sem=sent.at[s, there], recv_sem=got.at[s, there],
            device_id=plane_target(lax.div(there, NY), z_hi, lax.rem(there, NY)),
            device_id_type=MESH,
        )

    def to_self(source, into, s, got):
        return pltpu.make_async_copy(
            source.at[place_rows(s, here)], into.at[place_rows(s, here)], got.at[s, here]
        )

    def start_plane(source, into, s, there, sent, got):
        @pl.when(there != here)
        def _():
            to_plane(source, into, s, there, sent, got).start()

        @pl.when(there == here)
        def _():
            to_self(source, into, s, got).start()

    def wait_plane(source, into, s, there, sent, got):
        @pl.when(there != here)
        def _():
            from_plane(source, into, s, there, sent, got).wait_recv()

        @pl.when(there == here)
        def _():
            to_self(source, into, s, got).wait()

    def row_codes(shape, axis):
        row = lax.broadcasted_iota(jnp.int32, shape, axis)
        band = NY * CAP
        code = row + z_hi * band
        for edge in range(1, NX):
            code = code + jnp.where(row >= edge * band, band, 0)
        return code

    def dispatch(s, tok_view, cot_view, info):
        codes = row_codes((side_rows, tok), 0)
        hits = [
            jnp.where(codes == info[k : k + 1, 0:tok].astype(jnp.int32), 1.0, 0.0).astype(BF)
            for k in range(2)
        ]
        gather_x[...] = jnp.dot(
            hits[0] + hits[1], tok_view[...], preferred_element_type=F32
        ).astype(BF)
        cot = cot_view[...].astype(F32)
        scaled = [
            (column_of(info[k + 2 : k + 3, 0:tok]) * cot).astype(BF) for k in range(2)
        ]
        gather_dy[...] = (
            jnp.dot(hits[0], scaled[0], preferred_element_type=F32)
            + jnp.dot(hits[1], scaled[1], preferred_element_type=F32)
        ).astype(BF)

        @pl.loop(0, plane // 4)
        def _(step):
            g = lax.rem(step + 2 * x, plane // 4)
            rows = pl.ds(pl.multiple_of(g * message, 16), message)
            stacked = jnp.concatenate(
                [
                    gather_x[rows, 0:wide], gather_x[rows, wide:width],
                    gather_dy[rows, 0:wide], gather_dy[rows, wide:width],
                ],
                axis=0,
            )
            into = pl.ds(pl.multiple_of((s * plane // 4 + g) * group, 16), group)
            send[into, :] = jnp.dot(
                fold_ref[1], stacked, preferred_element_type=F32
            ).astype(BF)
            for j in range(4):
                start_plane(send, land, s, g * 4 + j, s_xy, r_xy)

    def group_at(spot_at):
        column = lax.rem(x + NX - lax.div(spot_at, 2), NX)
        return column * 2 + lax.rem(spot_at, 2)

    def unfold(stage):
        s = stage // 2

        @pl.loop(0, plane // 8)
        def _(i):
            spot_at = (stage % 2) * (plane // 8) + i
            g = group_at(spot_at)
            for j in range(4):
                wait_plane(send, land, s, g * 4 + j, s_xy, r_xy)
            here_rows = pl.ds(pl.multiple_of((s * plane // 4 + g) * group, 16), group)
            out = jnp.dot(fold_ref[0], land[here_rows, :], preferred_element_type=F32).astype(BF)
            into = pl.ds(pl.multiple_of((s * plane // 4 + spot_at) * message, 16), message)
            rows_x[into, 0:wide] = out[0:message]
            rows_x[into, wide:width] = out[message : 2 * message]
            rows_dy[into, 0:wide] = out[2 * message : 3 * message]
            rows_dy[into, wide:width] = out[3 * message : 4 * message]

    def own_rows(f, k, which):
        start = lax.div(k, blocks) * stage_rows + which * (stage_rows // 2) + f * part_rows
        return pl.ds(pl.multiple_of(start, 16), part_rows)

    def buf_rows(f, k):
        start = lax.div(k, blocks) * (stage_rows // 2) + f * part_rows
        return pl.ds(pl.multiple_of(start, 16), part_rows)

    def block_of(k):
        return lax.rem(k, blocks)

    def send_sib(f, k):
        return pltpu.make_async_remote_copy(
            src_ref=part.at[block_of(k), own_rows(f, k, 1 - core)],
            dst_ref=from_sib.at[block_of(k), buf_rows(f, k)],
            send_sem=s_sib.at[f, k], recv_sem=r_sib.at[f, k],
            device_id=sib, device_id_type=MESH,
        )

    def send_rs(f, k):
        return pltpu.make_async_remote_copy(
            src_ref=part.at[block_of(k), own_rows(f, k, core)],
            dst_ref=from_prev.at[block_of(k), buf_rows(f, k)],
            send_sem=s_rs.at[f, k], recv_sem=r_rs.at[f, k],
            device_id={"dp": me + 2 if f == 0 else me - 2}, device_id_type=MESH,
        )

    def send_done(f, k, target, sent, got):
        here_done = done.at[block_of(k), own_rows(f, k, core)]
        return pltpu.make_async_remote_copy(
            src_ref=here_done, dst_ref=here_done, send_sem=sent.at[f, k], recv_sem=got.at[f, k],
            device_id=target, device_id_type=MESH,
        )

    def send_ag(f, k):
        return send_done(f, k, {"dp": me - 2 if f == 0 else me + 2}, s_ag, r_ag)

    def send_fin(f, k):
        return send_done(f, k, sib, s_fin, r_fin)

    def parts(stage, h):
        rows = pl.ds(stage * stage_rows, stage_rows)
        cols = pl.ds(pl.multiple_of(h * BLOCK, BLOCK), BLOCK)
        part[h, rows, 0:BLOCK] = jnp.dot(
            rows_x[rows, :], wg_ref[:, cols], preferred_element_type=F32
        ).astype(BF)
        part[h, rows, BLOCK : 2 * BLOCK] = jnp.dot(
            rows_x[rows, :], wu_ref[:, cols], preferred_element_type=F32
        ).astype(BF)
        part[h, rows, 2 * BLOCK : 3 * BLOCK] = dot_last(rows_dy[rows, :], wd_ref[cols, :]).astype(BF)
        for f in range(2):
            send_sib(f, stage * blocks + h).start()

    def step(tick):
        for f in range(2):
            q = chip if f == 0 else last - chip
            k = tick - 1 - LAG * q

            @pl.when((k >= 0) & (k < count))
            def _():
                send_sib(f, k).wait_recv()
                mine = own_rows(f, k, core)
                h = block_of(k)
                buf = buf_rows(f, k)

                @pl.when(q == 0)
                def _():
                    part[h, mine, :] = (
                        part[h, mine, :].astype(F32) + from_sib[h, buf, :].astype(F32)
                    ).astype(BF)

                @pl.when(q > 0)
                def _():
                    send_rs(f, k).wait_recv()

                @pl.when((q > 0) & (q < last))
                def _():
                    part[h, mine, :] = (
                        part[h, mine, :].astype(F32)
                        + from_sib[h, buf, :].astype(F32)
                        + from_prev[h, buf, :].astype(F32)
                    ).astype(BF)

                @pl.when(q < last)
                def _():
                    send_rs(f, k).start()

                @pl.when(q == last)
                def _():
                    sums = []
                    for c in range(3):
                        cols = pl.ds(c * BLOCK, BLOCK)
                        sums.append(
                            part[h, mine, cols].astype(F32)
                            + from_sib[h, buf, cols].astype(F32)
                            + from_prev[h, buf, cols].astype(F32)
                        )
                    for c, value in enumerate(swiglu_back(*sums)):
                        done[h, mine, pl.ds(c * BLOCK, BLOCK)] = value
                    send_ag(f, k).start()
                    send_fin(f, k).start()

        for f in range(2):
            q = chip if f == 0 else last - chip
            k = tick - 1 - LAG * (2 * last - q)

            @pl.when((q < last) & (k >= 0) & (k < count))
            def _():
                send_ag(f, k).wait_recv()

                @pl.when(q > 0)
                def _():
                    send_ag(f, k).start()

                send_fin(f, k).start()

    def wait_fin(k):
        for f in range(2):
            send_fin(f, k).wait_recv()

    def send_back(stage):
        side = stage // 2
        rows = pl.ds(stage * stage_rows, stage_rows)
        total = None
        for h in range(blocks):
            cols = pl.ds(h * BLOCK, BLOCK)
            term = dot_last(done[h, rows, BLOCK : 2 * BLOCK], wg_ref[:, cols]) + dot_last(
                done[h, rows, 2 * BLOCK : 3 * BLOCK], wu_ref[:, cols]
            )
            total = term if total is None else total + term
        route[...] = total.astype(BF)

        @pl.loop(0, plane // 8)
        def _(i):
            g = group_at((stage % 2) * (plane // 8) + i)
            block = pl.ds(pl.multiple_of(i * message, 16), message)
            stacked = jnp.concatenate(
                [route[block, p * thin : (p + 1) * thin] for p in range(4)], axis=0
            )
            into = pl.ds(pl.multiple_of((side * plane // 4 + g) * group, 16), group)
            back_send[into, :] = jnp.dot(
                fold_ref[1], stacked, preferred_element_type=F32
            ).astype(BF)
            for j in range(4):
                start_plane(back_send, back_land, side, g * 4 + j, s_back, r_back)

    def combine(side, info):
        @pl.loop(0, plane // 4)
        def _(g):
            for j in range(4):
                wait_plane(back_send, back_land, side, g * 4 + j, s_back, r_back)
            block = pl.ds(pl.multiple_of((side * plane // 4 + g) * group, 16), group)
            out = jnp.dot(fold_ref[0], back_land[block, :], preferred_element_type=F32).astype(BF)
            into = pl.ds(pl.multiple_of(g * message, 16), message)
            for p in range(4):
                returned[into, p * thin : (p + 1) * thin] = out[p * message : (p + 1) * message]

        codes = row_codes((tok, side_rows), 1)
        hits = None
        for k in range(2):
            hit = codes == column_of(info[k : k + 1, 0:tok]).astype(jnp.int32)
            hits = hit if hits is None else hits | hit
        return jnp.dot(
            jnp.where(hits, 1.0, 0.0).astype(BF), returned[...], preferred_element_type=F32
        )

    for load in loads[3:6]:
        load.wait()
    dispatch(0, tok_ref, cot_ref, meta)
    meta_copy.wait_recv()
    crossing(0).wait_recv()
    crossing(1).wait_recv()
    dispatch(1, far.at[0], far.at[1], far_meta)

    def pair_dy_copy(stage):
        rows = pl.ds(stage * stage_rows, stage_rows)
        return pltpu.make_async_remote_copy(
            src_ref=rows_dy.at[rows], dst_ref=pair_dy.at[rows],
            send_sem=s_pdy.at[stage], recv_sem=r_pdy.at[stage],
            device_id=pair, device_id_type=MESH,
        )

    half_rows = stage_rows // 2

    def core_half(stage):
        return pl.ds(pl.multiple_of(stage * stage_rows + core * half_rows, 16), half_rows)

    def pair_hid_copy(stage):
        return pltpu.make_async_remote_copy(
            src_ref=hid_send.at[pl.ds(stage * half_rows, half_rows)],
            dst_ref=pair_hid.at[core_half(stage)],
            send_sem=s_pair.at[stage], recv_sem=r_pair.at[stage],
            device_id=pair, device_id_type=MESH,
        )

    def share_half(stage):
        return pltpu.make_async_remote_copy(
            src_ref=pair_hid.at[core_half(stage)], dst_ref=pair_hid.at[core_half(stage)],
            send_sem=s_half.at[stage], recv_sem=r_half.at[stage],
            device_id=sib, device_id_type=MESH,
        )

    def send_hidden(stage):
        for h in range(blocks):
            hid_send[pl.ds(stage * half_rows, half_rows), pl.ds(h * BLOCK, BLOCK)] = done[
                h, core_half(stage), 0:BLOCK
            ]
        pair_hid_copy(stage).start()

    def pass_on(stage):
        pair_hid_copy(stage).wait_recv()
        share_half(stage).start()

    for load in loads[6:]:
        load.wait()
    drain = 1 + 2 * LAG * last
    stages = count // blocks

    def finish(stage):
        for h in range(blocks):
            wait_fin(stage * blocks + h)
        send_hidden(stage)
        send_back(stage)
        if stage > 0:
            pass_on(stage - 1)

    finished = 0
    tick = 0
    for stage in range(stages):
        unfold(stage)
        pair_dy_copy(stage).start()

        @pl.loop(0, blocks)
        def _(h):
            parts(stage, h)
            step(stage * blocks + h)

        tick += blocks
    while finished < stages - 1:
        stop = (finished + 1) * blocks + drain
        pl.loop(tick, stop)(step)
        tick = stop
        finish(finished)
        finished += 1

    pl.loop(tick, tick + blocks)(step)
    finish(stages - 1)

    @pl.loop(0, blocks)
    def _(h):
        rows = pl.ds(pl.multiple_of(h * BLOCK, BLOCK), BLOCK)
        own[rows, :] = dot_first(done[h, :, 0:BLOCK], rows_dy[...])

    cross = pltpu.make_async_remote_copy(
        src_ref=cross_send, dst_ref=cross_land, send_sem=s_cross, recv_sem=r_cross,
        device_id=across, device_id_type=MESH,
    )
    partial[...] = combine(0, meta)
    pass_on(stages - 1)
    meta_copy.wait_send()
    for d in range(2):
        crossing(d).wait_send()

    @pl.loop(1, plane)
    def _(hop):
        there = lax.rem(here + hop, plane)
        for s in range(2):
            to_plane(send, land, s, there, s_xy, r_xy).wait_send()
        to_plane(back_send, back_land, 0, there, s_back, r_back).wait_send()

    @pl.loop(0, count)
    def _(k):
        for f in range(2):
            q = chip if f == 0 else last - chip
            send_sib(f, k).wait_send()
            send_fin(f, k).wait_send()

            @pl.when(q < last)
            def _():
                send_rs(f, k).wait_send()

            @pl.when(q > 0)
            def _():
                send_ag(f, k).wait_send()

    for stage in range(stages):
        pair_dy_copy(stage).wait_send()
        pair_hid_copy(stage).wait_send()

    cross_send[...] = combine(1, far_meta).astype(BF)
    cross.start()

    hot = jnp.max(
        jnp.where(hot_ref[...] == lax.rem(spot, plane), 1.0, 0.0), axis=1, keepdims=True
    )

    for stage in range(stages):
        pair_dy_copy(stage).wait_recv()
        share_half(stage).wait_recv()

    @pl.loop(0, blocks)
    def _(h):
        rows = pl.ds(pl.multiple_of(h * BLOCK, BLOCK), BLOCK)
        theirs = dot_first(pair_hid[:, rows], pair_dy[...])
        grad_down_ref[rows, :] = (own[rows, :] + hot * theirs).astype(BF)

    cross.wait_recv()
    grad_tok_ref[...] = (partial[...] + cross_land[...].astype(F32)).astype(BF)

    cross.wait_send()

    @pl.loop(1, plane)
    def _(hop):
        there = lax.rem(here + hop, plane)
        to_plane(back_send, back_land, 1, there, s_back, r_back).wait_send()

    for stage in range(stages):
        share_half(stage).wait_send()


def on_device(
    tokens, cotangent, gate_scale, expert_ids, expert_slots, hot_pairs, w_gate, w_up, w_down
):
    tok, width = tokens.shape
    hid = w_gate.shape[2]
    plane = NX * NY
    side_rows = plane * CAP
    rows = 2 * side_rows
    message = 4 * CAP
    blocks = hid // BLOCK
    count = 4 * blocks
    dma = pltpu.SemaphoreType.DMA
    flow = [dma((2, count))] * 8
    grad_tokens, grad_down = pl.pallas_call(
        layer_kernel,
        out_shape=(
            jax.ShapeDtypeStruct((tok, width), BF),
            jax.ShapeDtypeStruct((hid, width), BF),
        ),
        in_specs=[pl.BlockSpec(memory_space=pltpu.HBM)] * 9,
        out_specs=[pl.BlockSpec(memory_space=pltpu.VMEM)] * 2,
        scratch_shapes=[
            pltpu.VMEM(expert_ids.shape[::-1], jnp.int32),
            pltpu.VMEM(expert_slots.shape[::-1], jnp.int32),
            pltpu.VMEM(gate_scale.shape[::-1], F32),
            pltpu.VMEM((tok, width), BF),
            pltpu.VMEM((tok, width), BF),
            pltpu.VMEM((1, hot_pairs.shape[0]), jnp.int32),
            pltpu.VMEM((2, 16 * CAP, 16 * CAP), BF),
            pltpu.VMEM((width, hid), BF),
            pltpu.VMEM((width, hid), BF),
            pltpu.VMEM((hid, width), BF),
            pltpu.VMEM((2, tok, width), BF),
            pltpu.VMEM((8, 256), F32),
            pltpu.VMEM((8, 256), F32),
            pltpu.VMEM((side_rows, width), BF),
            pltpu.VMEM((side_rows, width), BF),
            pltpu.VMEM((2 * plane * message, width // 2), BF),
            pltpu.VMEM((2 * plane * message, width // 2), BF),
            pltpu.VMEM((rows, width), BF),
            pltpu.VMEM((rows, width), BF),
            pltpu.VMEM((blocks, rows, 3 * BLOCK), BF),
            pltpu.VMEM((blocks, side_rows, 3 * BLOCK), BF),
            pltpu.VMEM((blocks, side_rows, 3 * BLOCK), BF),
            pltpu.VMEM((blocks, rows, 3 * BLOCK), BF),
            pltpu.VMEM((side_rows // 2, width), BF),
            pltpu.VMEM((2 * plane * message, width // 4), BF),
            pltpu.VMEM((2 * plane * message, width // 4), BF),
            pltpu.VMEM((side_rows, width), BF),
            pltpu.VMEM((tok, width), F32),
            pltpu.VMEM((tok, width), BF),
            pltpu.VMEM((tok, width), BF),
            pltpu.VMEM((hid, width), F32),
            pltpu.VMEM((side_rows, hid), BF),
            pltpu.VMEM((rows, hid), BF),
            pltpu.VMEM((rows, width), BF),
            dma((2,)), dma((2,)), dma, dma, dma((2, plane)), dma((2, plane)),
        ] + flow + [
            dma((2, plane)), dma((2, plane)), dma, dma, dma((4,)), dma((4,)),
            dma((4,)), dma((4,)), dma((4,)), dma((4,)), dma((9,)),
        ],
        compiler_params=pltpu.CompilerParams(
            collective_id=0, has_side_effects=True, vmem_limit_bytes=52 * 1024 * 1024
        ),
        cost_estimate=pl.CostEstimate(
            flops=12 * rows * width * hid, bytes_accessed=8 * 1024 * 1024, transcendentals=0
        ),
        name="layer_backward",
    )(
        tokens, cotangent, gate_scale.T, expert_ids.T, expert_slots.T, hot_pairs.reshape(1, -1),
        w_gate[0], w_up[0], w_down[0],
    )
    return grad_tokens, grad_down[None]


def solution(mesh):
    placed = (
        P("expert", "dp"),
        P("expert", "dp"),
        P("expert", None),
        P("expert", None),
        P(),
        P(),
        P("expert", "dp", None),
        P("expert", "dp", None),
        P("expert", None, "dp"),
    )
    return jax.shard_map(
        on_device,
        mesh=mesh,
        in_specs=placed,
        out_specs=(P("expert", "dp"), P("expert", None, "dp")),
        check_vma=False,
    )
```
